512 devices in a mesh: illum: 32 (over z_hi, y), gx: 4 (over x), gy: 4 (over z_lo, core).
Axes of the slice: x: 4, y: 8, z: 8 (z_hi: 4, z_lo: 2; z = z_hi * 2 + z_lo), core: 2. Of those that a mesh axis runs over, the one named last changes fastest.
Arguments:
- density: float32 [128, 64, 128], P('gx', 'gy'), may hold values from 0 to 1
- moment_one: float32 [128, 64, 128], P('gx', 'gy'), may hold values from -0.6 to 0.6
- moment_two: float32 [128, 64, 128], P('gx', 'gy'), may hold values from 0.0002 to 0.0006
- forward_field: bfloat16 [32, 2, 3, 128, 64, 128], P('illum', None, None, 'gx', 'gy'), may hold values from -6 to 6
- adjoint_field: bfloat16 [32, 2, 3, 128, 64, 128], P('illum', None, None, 'gx', 'gy'), may hold values from -6 to 6
- objective_weight: float32 [32], P('illum'), may hold values from 0.02 to 0.2
Outputs:
- new_density: float32 [128, 64, 128], P('gx', 'gy')
- new_moment_one: float32 [128, 64, 128], P('gx', 'gy')
- new_moment_two: float32 [128, 64, 128], P('gx', 'gy')
- physical: float32 [128, 64, 128], P('gx', 'gy')
The draws below stay inside these ranges and needn't reach their ends.
All inputs are finite; a program needn't handle non-finite values.
Results may differ from the reference program's by a relative error of at most 0.0003.
Values sent between devices are 32-bit elements; how exact they have to be, the bound alone decides.
No kernel may reach another device: no remote copies, remote signals or barrier semaphores. Data moves between devices by JAX's collectives and lax.ppermute only.
A program may use at most 64 MiB of HBM per device.

```python
import math
import jax
import jax.numpy as jnp
from jax import lax

RADIUS = 8
SOURCES = 32
NX = 128
NY = 64
NZ = 128


def level_of(stream_key, shape, cuts, smallest, largest):
    gain, own = 1.0, jax.random.fold_in(stream_key, 6)
    for dim, shards_of in cuts:
        heights = jnp.exp(jax.random.uniform(jax.random.fold_in(own, dim), (shards_of,), jnp.float32, smallest / len(cuts), largest / len(cuts)))
        gain = gain * jnp.repeat(heights, shape[dim] // shards_of).reshape([-1 if axis == dim else 1 for axis in range(len(shape))])
    return gain


def normal_values(own_key, dims, width, most, split=(), kind=jnp.bfloat16):
    array = width * jax.random.normal(own_key, dims, jnp.float32)
    if split:
        array = array * level_of(own_key, dims, split, -0.22, 0.18)
    return jnp.clip(array, -most, most).astype(kind)


def setup_inputs(seed: int = 0) -> dict:
    key_list = jax.random.split(jax.random.key(seed), 7)
    return {
        "density": jnp.clip(1.0 * jax.random.uniform(key_list[0], (NX, NY, NZ), jnp.float32) ** level_of(key_list[0], (NX, NY, NZ), ((0, 4), (1, 4)), -0.2, 0.2), 0.0, 1.0),
        "moment_one": jnp.clip(jax.random.uniform(key_list[1], (NX, NY, NZ), jnp.float32, -0.6, 0.6) * level_of(key_list[1], (NX, NY, NZ), ((0, 4), (1, 4)), -0.4, 0.0), -0.6, 0.6),
        "moment_two": jnp.clip(jnp.exp(math.log(0.0006) - 1.09861236 * jax.random.uniform(key_list[2], (NX, NY, NZ), jnp.float32) ** level_of(key_list[2], (NX, NY, NZ), ((0, 4), (1, 4)), -0.2, 0.2)), 0.0002, 0.0006),
        "forward_field": normal_values(key_list[3], (SOURCES, 2, 3, NX, NY, NZ), 1.0, 6.0, ((0, 32), (3, 4), (4, 4))),
        "adjoint_field": normal_values(key_list[4], (SOURCES, 2, 3, NX, NY, NZ), 1.0, 6.0, ((0, 32), (3, 4), (4, 4))),
        "objective_weight": jnp.clip(jnp.exp(math.log(0.2) - 2.3025851 * jax.random.uniform(key_list[5], (SOURCES,), jnp.float32) ** level_of(key_list[5], (SOURCES,), ((0, 32),), -0.2, 0.2)), 0.02, 0.2),
    }


sharpness = 8.0
threshold = 0.5

def tap_weights():
    offsets = jnp.arange(-RADIUS, RADIUS + 1)
    return ((RADIUS + 1 - jnp.abs(offsets)) / (RADIUS + 1) ** 2).astype(jnp.float32)

def band_matrix(length):
    rows = jnp.arange(length)[:, None]
    cols = jnp.arange(length)[None, :]
    apart = jnp.abs(rows - cols)
    values = (RADIUS + 1 - apart).astype(jnp.float32) / float((RADIUS + 1) ** 2)
    return jnp.where(apart <= RADIUS, values, jnp.float32(0.0))

def line_filter(padded, axis, length):
    weights = tap_weights()
    total = jnp.zeros(padded.shape[:axis] + (length,) + padded.shape[axis + 1:], jnp.float32)
    for offset in range(2 * RADIUS + 1):
        total = total + weights[offset] * lax.slice_in_dim(padded, offset, offset + length, axis=axis)
    return total

def depth_filter(field):
    shape = field.shape
    flat = field.reshape(-1, shape[2])
    out = jnp.dot(flat, band_matrix(shape[2]), precision=lax.Precision.HIGHEST, preferred_element_type=jnp.float32)
    return out.reshape(shape)

def full_filter(field):
    padded = jnp.pad(field, ((RADIUS, RADIUS), (RADIUS, RADIUS), (0, 0)))
    along_x = line_filter(padded, 0, field.shape[0])
    along_y = line_filter(along_x, 1, field.shape[1])
    return depth_filter(along_y)

def project(value):
    scale = jnp.tanh(sharpness * threshold) + jnp.tanh(sharpness * (1.0 - threshold))
    return (jnp.tanh(sharpness * threshold) + jnp.tanh(sharpness * (value - threshold))) / scale

def slope(value):
    scale = jnp.tanh(sharpness * threshold) + jnp.tanh(sharpness * (1.0 - threshold))
    inner = jnp.tanh(sharpness * (value - threshold))
    return sharpness * (1.0 - inner * inner) / scale

def reference(density, moment_one, moment_two, forward_field, adjoint_field, objective_weight):
    filtered = full_filter(density)

    def one_source(items):
        fwd, adj, weight = items
        fwd = fwd.astype(jnp.float32)
        adj = adj.astype(jnp.float32)
        intersection = lax.optimization_barrier(jnp.sum(fwd[0] * adj[0] - fwd[1] * adj[1], axis=0))
        return weight * intersection
    terms = lax.map(one_source, (forward_field, adjoint_field, objective_weight))
    sensitivity = lax.optimization_barrier(jnp.sum(terms, axis=0))
    chained = sensitivity * slope(filtered)
    gradient = full_filter(chained)
    new_moment_one = 0.9 * moment_one + 0.1 * gradient
    new_moment_two = 0.999 * moment_two + 0.001 * gradient * gradient
    first_fix = 1.0 - 0.9 ** 5
    second_fix = 1.0 - 0.999 ** 5
    step = new_moment_one / first_fix / (jnp.sqrt(new_moment_two / second_fix) + 1e-08)
    new_density = jnp.clip(density - 0.05 * step, 0.0, 1.0)
    physical = project(full_filter(new_density))
    return (new_density, new_moment_one, new_moment_two, physical)
```

```python
import functools

import jax
import jax.numpy as jnp
import numpy as np
from jax import lax
from jax.experimental import pallas as pl
from jax.experimental.pallas import tpu as pltpu
from jax.sharding import PartitionSpec as P

RADIUS = 8
TAPS = RADIUS + 1
UNIT = 1.0 / float(TAPS**2)
sharpness = 8.0
threshold = 0.5

GROUPS = 4
SLABS = 32
DEEP = 4


def call(kernel, out_shape, **more):
    return pl.pallas_call(
        kernel,
        out_shape=out_shape,
        compiler_params=pltpu.CompilerParams(vmem_limit_bytes=48 * 1024 * 1024),
        **more,
    )


def whole(count):
    return [pl.BlockSpec(memory_space=pltpu.VMEM)] * count


def hat(a, b):
    return jnp.maximum(TAPS - jnp.abs(a - b), 0)


def bf(value):
    return value.astype(jnp.bfloat16)


def f32(value):
    return value.astype(jnp.float32)


def parts_of(value, count):
    out = []
    for _ in range(count):
        part = bf(value)
        out.append(part)
        value = value - f32(part)
    return out


def dot(a, b, dims):
    return lax.dot_general(a, b, (dims, ((), ())), preferred_element_type=jnp.float32)


def iota(shape, dim):
    return lax.broadcasted_iota(jnp.int32, shape, dim)


def sensitivity_kernel(fwd_ref, adj_ref, weight_ref, density_ref, terms_ref, own_ref):
    slab = lax.axis_index("illum")
    total = None
    for component in range(3):
        real = f32(fwd_ref[0, 0, component]) * f32(adj_ref[0, 0, component])
        imag = f32(fwd_ref[0, 1, component]) * f32(adj_ref[0, 1, component])
        term = real - imag
        total = term if total is None else total + term
    total = (total * weight_ref[0]).reshape(256, 128)
    side = jnp.concatenate([total[:128], total[128:]], axis=1)
    rows, cols = iota((256, 256), 0), iota((256, 256), 1)
    group = ((rows >> 2) & 1) == (cols >> 7)
    depth = (rows >> 3) * DEEP + (rows & 3)
    pick = bf(jnp.where(group & (depth == (cols & 127)), 1.0, 0.0))
    turned = sum(dot(pick, part, ((1,), (1,))) for part in parts_of(side, 3))
    terms_ref[...] = turned.reshape(32, 8, 128)
    dens = density_ref[...].reshape(256, 128)
    dens = jnp.concatenate([dens[:128], dens[128:]], axis=1)
    rows, cols = iota((8, 256), 0), iota((8, 256), 1)
    near = hat(slab * DEEP + (rows & 3), cols & 127)
    band = bf(jnp.where(((rows >> 2) & 1) == (cols >> 7), near, 0).astype(jnp.float32))
    own_ref[...] = sum(dot(band, part, ((1,), (1,))) for part in parts_of(dens, 3))


def sensitivity(fwd, adj, weight, density):
    return call(
        sensitivity_kernel,
        (jax.ShapeDtypeStruct((SLABS, 16, 128), jnp.float32), jax.ShapeDtypeStruct((16, 128), jnp.float32)),
        grid=(2,),
        in_specs=[
            pl.BlockSpec((1, 2, 3, 16, 16, 128), lambda i: (0, 0, 0, i, 0, 0)),
            pl.BlockSpec((1, 2, 3, 16, 16, 128), lambda i: (0, 0, 0, i, 0, 0)),
            pl.BlockSpec(memory_space=pltpu.SMEM),
            pl.BlockSpec((16, 16, 128), lambda i: (i, 0, 0)),
        ],
        out_specs=(
            pl.BlockSpec((SLABS, 8, 128), lambda i: (0, i, 0)),
            pl.BlockSpec((8, 128), lambda i: (i, 0)),
        ),
    )(fwd, adj, weight, density)


def sum_kernel(terms_ref, own_ref, out_ref):
    both = jnp.concatenate([jnp.sum(terms_ref[...], axis=0), own_ref[...]], axis=0)
    out_ref[...] = jnp.broadcast_to(both[None], out_ref.shape)


def summed(terms, own):
    return call(
        sum_kernel,
        jax.ShapeDtypeStruct((16, 32, 128), jnp.float32),
        in_specs=whole(2),
        out_specs=whole(1)[0],
    )(terms, own)


def plane_taps():
    dx, dy, x, y = np.meshgrid(np.arange(-1, 2), np.arange(-1, 2), np.arange(8), np.arange(16), indexing="ij")
    far_x = (x + 8 * dx).reshape(-1, 1) - np.repeat(np.arange(8), 16)
    far_y = (y + 16 * dy).reshape(-1, 1) - np.tile(np.arange(16), 8)
    taps = np.maximum(TAPS - np.abs(far_x), 0) * np.maximum(TAPS - np.abs(far_y), 0)
    return jnp.asarray(taps.astype(np.float32)).astype(jnp.bfloat16)


PAD_X, PAD_Y = 3, 2


def slab_kernel(all_ref, taps_ref, out_ref, sens, dens):
    gx, gy = lax.axis_index("gx"), lax.axis_index("gy")
    low = iota((8, 128), 0) < DEEP
    zero = jnp.zeros((8, 128), jnp.float32)
    for ref in (sens, dens):
        for x in range(16 + 2 * PAD_X):
            for y in range(4 + 2 * PAD_Y):
                if not (PAD_X <= x < 16 + PAD_X and PAD_Y <= y < 4 + PAD_Y):
                    ref[x, y] = zero
    for x in range(4):
        for y in range(4):
            for pair in range(2):
                at = PAD_X + 4 * x + 2 * pair
                for ref, base in ((sens, 0), (dens, 16)):
                    tile = all_ref[4 * x + y, base + 8 * pair : base + 8 * pair + 8, :]
                    turned = pltpu.roll(tile, DEEP, 0)
                    twice = (jnp.where(low, tile, turned), jnp.where(low, turned, tile))
                    for odd in range(2):
                        value = twice[odd]
                        if base:
                            top = f32(bf(value))
                            value = jnp.where(low, top, value - top)
                        ref[at + odd, PAD_Y + y] = value
    taps = taps_ref[...]
    first = GROUPS * gx
    window = dens[pl.ds(first, 10), pl.ds(gy, 5)]
    side = jnp.concatenate(
        [bf(window[dx : dx + 8, dy : dy + 3].reshape(192, 128)) for dx in range(3) for dy in range(3)], axis=1
    )
    filtered = dot(side, taps, ((1,), (0,))).reshape(24, 8, 128)
    filtered = (filtered + pltpu.roll(filtered, DEEP, 1)) * (UNIT * UNIT * UNIT)
    inner = jnp.tanh(sharpness * (filtered - threshold))
    scale = jnp.tanh(jnp.full((8, 128), sharpness * threshold, jnp.float32)) * 2.0
    slope = sharpness * (1.0 - inner * inner) / scale
    chained = slope * sens[pl.ds(first + 1, 8), pl.ds(gy + 1, 3)].reshape(24, 8, 128)
    top = f32(bf(chained))
    chained = bf(jnp.where(low, top, chained - top)).reshape(8, 3, 8, 128)
    side = jnp.concatenate([chained[dx : dx + 6, dy].reshape(48, 128) for dx in range(3) for dy in range(3)], axis=1)
    result = dot(side, taps, ((1,), (0,))).reshape(6, 8, 128)
    result = result + pltpu.roll(result, DEEP, 1)
    for pair in range(3):
        tile = jnp.where(low, result[2 * pair], result[2 * pair + 1])
        out_ref[:, 8 * pair : 8 * pair + 8, :] = jnp.broadcast_to(tile[None], (SLABS, 8, 128))


def slab_step(everything):
    return call(
        slab_kernel,
        jax.ShapeDtypeStruct((SLABS, 24, 128), jnp.float32),
        in_specs=whole(2),
        out_specs=whole(1)[0],
        scratch_shapes=[pltpu.VMEM((16 + 2 * PAD_X, 4 + 2 * PAD_Y, 8, 128), jnp.float32)] * 2,
    )(everything, plane_taps())


def adam(density, moment_one, moment_two, gradient):
    new_one = 0.9 * moment_one + 0.1 * gradient
    new_two = 0.999 * moment_two + 0.001 * gradient * gradient
    first_fix = 1.0 - 0.9**5
    second_fix = 1.0 - 0.999**5
    step = new_one / first_fix / (jnp.sqrt(new_two / second_fix) + 1e-08)
    return jnp.clip(density - 0.05 * step, 0.0, 1.0), new_one, new_two


def box(value):
    n = value.shape[0]
    two = value[: n - 1] + value[1:]
    four = two[: n - 3] + two[2:]
    eight = four[: n - 7] + four[4:]
    return eight[: n - 8] + value[8:]


def adam_kernel(slabs_ref, d_ref, m_ref, v_ref, left_ref, right_ref, nd_ref, nm_ref, nv_ref, fx_ref, lo_ref, hi_ref, ext):
    gx = lax.axis_index("gx")
    rows, cols = iota((256, 256), 0), iota((256, 256), 1)
    depth = (rows >> 3) * DEEP + (rows & 3)
    near = jnp.where(((rows >> 2) & 1) == (cols >> 7), hat(depth, cols & 127), 0)
    band = bf(near.astype(jnp.float32))
    for pair in range(3):
        side = slabs_ref[:, 8 * pair : 8 * pair + 8, :].reshape(256, 128)
        both = sum(dot(part, band, ((0,), (0,))) for part in parts_of(side, 2)) * (UNIT * UNIT * UNIT)
        for odd in range(2):
            group = 2 * pair + odd - 1
            gradient = both[:, 128 * odd : 128 * odd + 128].reshape(8, 16, 128)
            if group == -1:
                new, _, _ = adam(left_ref[0], left_ref[1], left_ref[2], gradient)
                new = jnp.where(gx > 0, new, 0.0)
            elif group == GROUPS:
                new, _, _ = adam(right_ref[0], right_ref[1], right_ref[2], gradient)
                new = jnp.where(gx < lax.axis_size("gx") - 1, new, 0.0)
            else:
                at = slice(8 * group, 8 * group + 8)
                new, one, two = adam(d_ref[at], m_ref[at], v_ref[at], gradient)
                nd_ref[at] = new
                nm_ref[at] = one
                nv_ref[at] = two
            ext[8 * (group + 1) : 8 * (group + 1) + 8] = new
    along_x = box(box(ext[...])) * UNIT
    fx_ref[...] = along_x
    lo_ref[...] = along_x[:, :8]
    hi_ref[...] = along_x[:, 8:]


def adam_step(slabs, density, moment_one, moment_two, left, right):
    tile = jax.ShapeDtypeStruct((32, 16, 128), jnp.float32)
    half = jax.ShapeDtypeStruct((32, 8, 128), jnp.float32)
    return call(
        adam_kernel,
        (tile, tile, tile, tile, half, half),
        in_specs=whole(6),
        out_specs=tuple(whole(6)),
        scratch_shapes=[pltpu.VMEM((48, 16, 128), jnp.float32)],
    )(slabs, density, moment_one, moment_two, left, right)


def physical_kernel(fx_ref, before_ref, after_ref, out_ref):
    rows, cols = iota((128, 256), 0), iota((128, 256), 1)
    own = cols - 64
    late = cols - 192
    before, after = cols < 64, cols >= 192
    x = jnp.where(before, cols >> 3, jnp.where(after, late >> 3, own >> 4))
    y = jnp.where(before, (cols & 7) - 8, jnp.where(after, (late & 7) + 16, own & 15))
    spread = bf(jnp.where(x == (rows >> 4), hat(y, rows & 15), 0).astype(jnp.float32))
    band = bf(hat(iota((128, 128), 0), iota((128, 128), 1)).astype(jnp.float32))
    scale = jnp.tanh(jnp.full((128, 128), sharpness * threshold, jnp.float32))
    for pair in range(2):
        sides = []
        for odd in range(2):
            at = slice(8 * (2 * pair + odd), 8 * (2 * pair + odd) + 8)
            sides.append(
                jnp.concatenate(
                    [
                        before_ref[at].reshape(64, 128),
                        fx_ref[at].reshape(128, 128),
                        after_ref[at].reshape(64, 128),
                    ],
                    axis=0,
                )
            )
        side = jnp.concatenate(sides, axis=1)
        both = sum(dot(spread, part, ((1,), (0,))) for part in parts_of(side, 2))
        for odd in range(2):
            at = slice(8 * (2 * pair + odd), 8 * (2 * pair + odd) + 8)
            along_y = both[:, 128 * odd : 128 * odd + 128]
            value = sum(dot(part, band, ((1,), (0,))) for part in parts_of(along_y, 2)) * (UNIT * UNIT)
            value = (scale + jnp.tanh(sharpness * (value - threshold))) / (scale + scale)
            out_ref[at] = value.reshape(8, 16, 128)


def physical_step(along_x, before, after):
    return call(
        physical_kernel,
        jax.ShapeDtypeStruct((32, 16, 128), jnp.float32),
        in_specs=whole(3),
        out_specs=whole(1)[0],
    )(along_x, before, after)


def neighbours(last, leading, axis):
    size = lax.axis_size(axis)
    up = [(i, i + 1) for i in range(size - 1)]
    down = [(j, i) for i, j in up]
    return lax.ppermute(last, axis, up), lax.ppermute(leading, axis, down)


def exchange(value, axes):
    return lax.all_to_all(value, axes, 0, 0, tiled=True)


def shards(density, moment_one, moment_two, forward_field, adjoint_field, objective_weight):
    stacked = jnp.stack([density, moment_one, moment_two])
    left, right = neighbours(stacked[:, 24:], stacked[:, :8], "gx")
    terms, own = sensitivity(forward_field, adjoint_field, objective_weight, density)
    terms = exchange(terms, "illum")
    everything = exchange(summed(terms, own), ("gx", "gy"))
    slabs = exchange(slab_step(everything), "illum")
    new_density, new_one, new_two, along_x, leading, last = adam_step(
        slabs, density, moment_one, moment_two, left, right
    )
    before, after = neighbours(last, leading, "gy")
    physical = physical_step(along_x, before, after)
    return (new_density, new_one, new_two, physical)


def solution(mesh):
    tile = P("gx", "gy", None)
    field = P("illum", None, None, "gx", "gy", None)
    return jax.shard_map(
        shards,
        mesh=mesh,
        in_specs=(tile, tile, tile, field, field, P("illum")),
        out_specs=(tile, tile, tile, tile),
        check_vma=False,
    )
```

```python
import jax
import jax.numpy as jnp
import numpy as np
from jax import lax
from jax.experimental import pallas as pl
from jax.experimental.pallas import tpu as pltpu
from jax.sharding import PartitionSpec as P

RADIUS = 8
TAPS = RADIUS + 1
UNIT = 1.0 / float(TAPS**2)
sharpness = 8.0
threshold = 0.5

GROUPS = 4
SLABS = 32
DEEP = 4


def call(kernel, out_shape, limit=48 * 1024 * 1024, **more):
    return pl.pallas_call(
        kernel,
        out_shape=out_shape,
        compiler_params=pltpu.CompilerParams(vmem_limit_bytes=limit),
        **more,
    )


def in_hbm(value):
    return pltpu.with_memory_space_constraint(value, pltpu.HBM)


def whole(count):
    return [pl.BlockSpec(memory_space=pltpu.VMEM)] * count


def hat(a, b):
    return jnp.maximum(TAPS - jnp.abs(a - b), 0)


def bf(value):
    return value.astype(jnp.bfloat16)


def f32(value):
    return value.astype(jnp.float32)


def parts_of(value, count):
    out = []
    for _ in range(count):
        part = bf(value)
        out.append(part)
        value = value - f32(part)
    return out


def dot(a, b, dims):
    return lax.dot_general(a, b, (dims, ((), ())), preferred_element_type=jnp.float32)


def iota(shape, dim):
    return lax.broadcasted_iota(jnp.int32, shape, dim)


def sensitivity_kernel(fwd_ref, adj_ref, weight_ref, terms_ref, fwd, adj, sems):
    copies = []
    for group in range(GROUPS):
        for which, (source, target) in enumerate(((fwd_ref, fwd), (adj_ref, adj))):
            piece = source.at[0, :, :, pl.ds(8 * group, 8)]
            copies.append(pltpu.make_async_copy(piece, target.at[group], sems.at[2 * group + which]))
            copies[-1].start()
    low = iota((8, 128), 0) < DEEP
    for pair in range(2):
        sides = []
        for group in (2 * pair, 2 * pair + 1):
            copies[2 * group].wait()
            copies[2 * group + 1].wait()
            total = None
            for component in range(3):
                real = f32(fwd[group, 0, component]) * f32(adj[group, 0, component])
                imag = f32(fwd[group, 1, component]) * f32(adj[group, 1, component])
                total = real - imag if total is None else total + (real - imag)
            sides.append((total * weight_ref[0]).reshape(128, 128))
        even, odd = (side.T.reshape(16, 8, 128) for side in sides)
        first = jnp.where(low, even, pltpu.roll(odd, DEEP, 1))
        second = jnp.where(low, pltpu.roll(even, DEEP, 1), odd)
        tiles = jnp.stack([first, second], axis=1).reshape(SLABS, 8, 128)
        terms_ref[:, 8 * pair : 8 * pair + 8, :] = tiles


def sensitivity(fwd, adj, weight):
    hbm = pl.BlockSpec(memory_space=pltpu.HBM)
    held = pltpu.VMEM((GROUPS, 2, 3, 8, 16, 128), jnp.bfloat16)
    return call(
        sensitivity_kernel,
        jax.ShapeDtypeStruct((SLABS, 16, 128), jnp.float32),
        in_specs=[hbm, hbm, pl.BlockSpec(memory_space=pltpu.SMEM)],
        out_specs=whole(1)[0],
        scratch_shapes=[held, held, pltpu.SemaphoreType.DMA((2 * GROUPS,))],
    )(in_hbm(fwd), in_hbm(adj), weight)


def middle_kernel(terms_ref, d_ref, m_ref, v_ref, out_ref, near_ref, far_ref):
    slab = lax.axis_index("illum")
    rows, cols = iota((8, 256), 0), iota((8, 256), 1)
    near = hat(slab * DEEP + (rows & 3), cols & 127)
    band = bf(jnp.where(((rows >> 2) & 1) == (cols >> 7), near, 0).astype(jnp.float32))
    own = []
    for pair in range(2):
        dens = d_ref[16 * pair : 16 * pair + 16].reshape(256, 128)
        dens = jnp.concatenate([dens[:128], dens[128:]], axis=1)
        own.append(sum(dot(band, part, ((1,), (1,))) for part in parts_of(dens, 2)))
    both = jnp.concatenate([jnp.sum(terms_ref[...], axis=0)] + own, axis=0)
    out_ref[...] = jnp.broadcast_to(both[None], out_ref.shape)
    near_at = pl.multiple_of(24 * (1 - (lax.axis_index("gx") & 1)), 8)
    for k, ref in enumerate((d_ref, m_ref, v_ref)):
        near_ref[k] = ref[pl.ds(near_at, 8)]
        far_ref[k] = ref[pl.ds(24 - near_at, 8)]


def middle(terms, density, moment_one, moment_two):
    edge = jax.ShapeDtypeStruct((3, 8, 16, 128), jnp.float32)
    return call(
        middle_kernel,
        (jax.ShapeDtypeStruct((16, 32, 128), jnp.float32), edge, edge),
        in_specs=whole(4),
        out_specs=tuple(whole(3)),
    )(terms, density, moment_one, moment_two)


def plane_taps():
    dx, dy, x, y = np.meshgrid(np.arange(-1, 2), np.arange(-1, 2), np.arange(8), np.arange(16), indexing="ij")
    far_x = (x + 8 * dx).reshape(-1, 1) - np.repeat(np.arange(8), 16)
    far_y = (y + 16 * dy).reshape(-1, 1) - np.tile(np.arange(16), 8)
    taps = np.maximum(TAPS - np.abs(far_x), 0) * np.maximum(TAPS - np.abs(far_y), 0)
    return jnp.asarray(taps.astype(np.float32)).astype(jnp.bfloat16)


PAD_X, PAD_Y = 3, 2


def slab_kernel(all_ref, taps_ref, out_ref, sens, dens):
    gx, gy = lax.axis_index("gx"), lax.axis_index("gy")
    low = iota((8, 128), 0) < DEEP
    zero = jnp.zeros((8, 128), jnp.float32)
    for ref in (sens, dens):
        for x in range(16 + 2 * PAD_X):
            for y in range(4 + 2 * PAD_Y):
                if not (PAD_X <= x < 16 + PAD_X and PAD_Y <= y < 4 + PAD_Y):
                    ref[x, y] = zero
    for x in range(4):
        for y in range(4):
            for pair in range(2):
                at = PAD_X + 4 * x + 2 * pair
                for ref, base in ((sens, 0), (dens, 16)):
                    tile = all_ref[4 * x + y, base + 8 * pair : base + 8 * pair + 8, :]
                    turned = pltpu.roll(tile, DEEP, 0)
                    twice = (jnp.where(low, tile, turned), jnp.where(low, turned, tile))
                    for odd in range(2):
                        value = twice[odd]
                        if base:
                            top = f32(bf(value))
                            value = jnp.where(low, top, value - top)
                        ref[at + odd, PAD_Y + y] = value
    taps = taps_ref[...]
    first = GROUPS * gx
    window = dens[pl.ds(first, 10), pl.ds(gy, 5)]
    side = jnp.concatenate(
        [bf(window[dx : dx + 8, dy : dy + 3].reshape(192, 128)) for dx in range(3) for dy in range(3)], axis=1
    )
    filtered = dot(side, taps, ((1,), (0,))).reshape(24, 8, 128)
    filtered = (filtered + pltpu.roll(filtered, DEEP, 1)) * (UNIT * UNIT * UNIT)
    inner = jnp.tanh(sharpness * (filtered - threshold))
    scale = jnp.tanh(jnp.full((8, 128), sharpness * threshold, jnp.float32)) * 2.0
    slope = sharpness * (1.0 - inner * inner) / scale
    chained = slope * sens[pl.ds(first + 1, 8), pl.ds(gy + 1, 3)].reshape(24, 8, 128)
    top = f32(bf(chained))
    chained = bf(jnp.where(low, top, chained - top)).reshape(8, 3, 8, 128)
    side = jnp.concatenate([chained[dx : dx + 6, dy].reshape(48, 128) for dx in range(3) for dy in range(3)], axis=1)
    result = dot(side, taps, ((1,), (0,))).reshape(6, 8, 128)
    result = result + pltpu.roll(result, DEEP, 1)
    for pair in range(3):
        tile = jnp.where(low, result[2 * pair], result[2 * pair + 1])
        out_ref[:, 8 * pair : 8 * pair + 8, :] = jnp.broadcast_to(tile[None], (SLABS, 8, 128))


def slab_step(everything):
    return call(
        slab_kernel,
        jax.ShapeDtypeStruct((SLABS, 24, 128), jnp.float32),
        in_specs=whole(2),
        out_specs=whole(1)[0],
        scratch_shapes=[pltpu.VMEM((16 + 2 * PAD_X, 4 + 2 * PAD_Y, 8, 128), jnp.float32)] * 2,
    )(everything, plane_taps())


def adam(density, moment_one, moment_two, gradient):
    new_one = 0.9 * moment_one + 0.1 * gradient
    new_two = 0.999 * moment_two + 0.001 * gradient * gradient
    first_fix = 1.0 - 0.9**5
    second_fix = 1.0 - 0.999**5
    step = new_one / first_fix / (jnp.sqrt(new_two / second_fix) + 1e-08)
    return jnp.clip(density - 0.05 * step, 0.0, 1.0), new_one, new_two


def box(value):
    n = value.shape[0]
    two = value[: n - 1] + value[1:]
    four = two[: n - 3] + two[2:]
    eight = four[: n - 7] + four[4:]
    return eight[: n - 8] + value[8:]


def adam_kernel(slabs_ref, d_ref, m_ref, v_ref, near_ref, far_ref, nd_ref, nm_ref, nv_ref, fx_ref, ynear_ref, yfar_ref, ext):
    gx, gy = lax.axis_index("gx"), lax.axis_index("gy")
    even_x, even_y = (gx & 1) == 0, (gy & 1) == 0
    rows, cols = iota((256, 256), 0), iota((256, 256), 1)
    depth = (rows >> 3) * DEEP + (rows & 3)
    near = jnp.where(((rows >> 2) & 1) == (cols >> 7), hat(depth, cols & 127), 0)
    band = bf(near.astype(jnp.float32))
    for pair in range(3):
        side = slabs_ref[:, 8 * pair : 8 * pair + 8, :].reshape(256, 128)
        both = sum(dot(part, band, ((0,), (0,))) for part in parts_of(side, 2)) * (UNIT * UNIT * UNIT)
        for odd in range(2):
            group = 2 * pair + odd - 1
            gradient = both[:, 128 * odd : 128 * odd + 128].reshape(8, 16, 128)
            if group == -1:
                left = [jnp.where(even_x, far_ref[k], near_ref[k]) for k in range(3)]
                new, _, _ = adam(*left, gradient)
                new = jnp.where(gx > 0, new, 0.0)
            elif group == GROUPS:
                right = [jnp.where(even_x, near_ref[k], far_ref[k]) for k in range(3)]
                new, _, _ = adam(*right, gradient)
                new = jnp.where(gx < lax.axis_size("gx") - 1, new, 0.0)
            else:
                at = slice(8 * group, 8 * group + 8)
                new, one, two = adam(d_ref[at], m_ref[at], v_ref[at], gradient)
                nd_ref[at] = new
                nm_ref[at] = one
                nv_ref[at] = two
            ext[8 * (group + 1) : 8 * (group + 1) + 8] = new
    along_x = box(box(ext[...])) * UNIT
    fx_ref[...] = along_x
    low, high = along_x[:, :8], along_x[:, 8:]
    ynear_ref[...] = jnp.where(even_y, high, low)
    yfar_ref[...] = jnp.where(even_y, low, high)


def adam_step(slabs, density, moment_one, moment_two, near, far):
    tile = jax.ShapeDtypeStruct((32, 16, 128), jnp.float32)
    half = jax.ShapeDtypeStruct((32, 8, 128), jnp.float32)
    return call(
        adam_kernel,
        (tile, tile, tile, tile, half, half),
        in_specs=whole(6),
        out_specs=tuple(whole(6)),
        scratch_shapes=[pltpu.VMEM((48, 16, 128), jnp.float32)],
    )(slabs, density, moment_one, moment_two, near, far)


def yz_filter(spread, sides):
    band = bf(hat(iota((128, 128), 0), iota((128, 128), 1)).astype(jnp.float32))
    side = jnp.concatenate(sides, axis=1)
    both = sum(dot(spread, part, ((1,), (0,))) for part in parts_of(side, 2))
    for odd in range(2):
        along_y = both[:, 128 * odd : 128 * odd + 128]
        yield sum(dot(part, band, ((1,), (0,))) for part in parts_of(along_y, 2)) * (UNIT * UNIT)


def own_kernel(fx_ref, nd_ref, nm_ref, nv_ref, own_ref, nd_out, nm_out, nv_out, sems):
    copies = [
        pltpu.make_async_copy(source, target, sems.at[k])
        for k, (source, target) in enumerate(((nd_ref, nd_out), (nm_ref, nm_out), (nv_ref, nv_out)))
    ]
    for copy in copies:
        copy.start()
    rows, cols = iota((128, 128), 0), iota((128, 128), 1)
    spread = bf(jnp.where((rows >> 4) == (cols >> 4), hat(rows & 15, cols & 15), 0).astype(jnp.float32))
    for pair in range(2):
        groups = [slice(8 * g, 8 * g + 8) for g in (2 * pair, 2 * pair + 1)]
        values = yz_filter(spread, [fx_ref[at].reshape(128, 128) for at in groups])
        for at, value in zip(groups, values):
            own_ref[at] = value.reshape(8, 16, 128)
    for copy in copies:
        copy.wait()


def own_step(along_x, *results):
    tile = jax.ShapeDtypeStruct((32, 16, 128), jnp.float32)
    return call(
        own_kernel,
        (tile, tile, tile, tile),
        in_specs=whole(4),
        out_specs=tuple(whole(1) + [pl.BlockSpec(memory_space=pltpu.HBM)] * 3),
        scratch_shapes=[pltpu.SemaphoreType.DMA((3,))],
    )(along_x, *results)


def physical_kernel(own_ref, near_ref, far_ref, out_ref, held, sems):
    even = (lax.axis_index("gy") & 1) == 0
    rows, cols = iota((128, 128), 0), iota((128, 128), 1)
    later = (cols < 64) == even
    y = (cols & 7) + jnp.where(later, 16, -8)
    spread = bf(jnp.where(((cols & 63) >> 3) == (rows >> 4), hat(y, rows & 15), 0).astype(jnp.float32))
    scale = jnp.tanh(jnp.full((128, 128), sharpness * threshold, jnp.float32))
    copies = []
    for pair in range(2):
        groups = [slice(8 * g, 8 * g + 8) for g in (2 * pair, 2 * pair + 1)]
        sides = [jnp.concatenate([near_ref[at].reshape(64, 128), far_ref[at].reshape(64, 128)], axis=0) for at in groups]
        for at, value in zip(groups, yz_filter(spread, sides)):
            value = value + own_ref[at].reshape(128, 128)
            value = (scale + jnp.tanh(sharpness * (value - threshold))) / (scale + scale)
            held[at] = value.reshape(8, 16, 128)
            copies.append(pltpu.make_async_copy(held.at[at], out_ref.at[at], sems.at[len(copies)]))
            copies[-1].start()
    for copy in copies:
        copy.wait()


def physical_step(own, near, far):
    return call(
        physical_kernel,
        jax.ShapeDtypeStruct((32, 16, 128), jnp.float32),
        in_specs=whole(3),
        out_specs=pl.BlockSpec(memory_space=pltpu.HBM),
        scratch_shapes=[pltpu.VMEM((32, 16, 128), jnp.float32), pltpu.SemaphoreType.DMA((GROUPS,))],
    )(own, near, far)


def swap(near, far, axis):
    size = lax.axis_size(axis)
    pairs = [(i, i ^ 1) for i in range(size)]
    others = [(i, j) for k in range(1, size - 1, 2) for i, j in ((k, k + 1), (k + 1, k))]
    return lax.ppermute(near, axis, pairs), lax.ppermute(far, axis, others)


def exchange(value, axes):
    return lax.all_to_all(value, axes, 0, 0, tiled=True)


def shards(density, moment_one, moment_two, forward_field, adjoint_field, objective_weight):
    state = (density, moment_one, moment_two)
    terms = exchange(sensitivity(forward_field, adjoint_field, objective_weight), "illum")
    both, near, far = middle(terms, *state)
    slab = slab_step(exchange(both, ("gx", "gy")))
    slab, near, far = lax.optimization_barrier((slab, near, far))
    slabs = exchange(slab, "illum")
    near, far = swap(near, far, "gx")
    *results, along_x, near, far = adam_step(slabs, *state, near, far)
    near, far = swap(near, far, "gy")
    own, *results = own_step(along_x, *results)
    return (*results, physical_step(own, near, far))


def solution(mesh):
    tile = P("gx", "gy", None)
    field = P("illum", None, None, "gx", "gy", None)
    return jax.shard_map(
        shards,
        mesh=mesh,
        in_specs=(tile, tile, tile, field, field, P("illum")),
        out_specs=(tile, tile, tile, tile),
        check_vma=False,
    )
```

```python
import jax
import jax.numpy as jnp
import numpy as np
from jax import lax
from jax.experimental import pallas as pl
from jax.experimental.pallas import tpu as pltpu
from jax.sharding import PartitionSpec as P

RADIUS = 8
TAPS = RADIUS + 1
UNIT = 1.0 / float(TAPS**2)
sharpness = 8.0
threshold = 0.5

GROUPS = 4
SLABS = 32
DEEP = 4


def call(kernel, out_shape, limit=48 * 1024 * 1024, **more):
    return pl.pallas_call(
        kernel,
        out_shape=out_shape,
        compiler_params=pltpu.CompilerParams(vmem_limit_bytes=limit),
        **more,
    )


def in_hbm(value):
    return pltpu.with_memory_space_constraint(value, pltpu.HBM)


def whole(count):
    return [pl.BlockSpec(memory_space=pltpu.VMEM)] * count


def hat(a, b):
    return jnp.maximum(TAPS - jnp.abs(a - b), 0)


def bf(value):
    return value.astype(jnp.bfloat16)


def f32(value):
    return value.astype(jnp.float32)


def parts_of(value, count):
    out = []
    for _ in range(count):
        part = bf(value)
        out.append(part)
        value = value - f32(part)
    return out


def dot(a, b, dims):
    return lax.dot_general(a, b, (dims, ((), ())), preferred_element_type=jnp.float32)


def iota(shape, dim):
    return lax.broadcasted_iota(jnp.int32, shape, dim)


def sensitivity_kernel(fwd_ref, adj_ref, weight_ref, terms_ref, fwd, adj, sems):
    copies = []
    for group in range(GROUPS):
        for which, (source, target) in enumerate(((fwd_ref, fwd), (adj_ref, adj))):
            piece = source.at[0, :, :, pl.ds(8 * group, 8)]
            copies.append(pltpu.make_async_copy(piece, target.at[group], sems.at[2 * group + which]))
            copies[-1].start()
    low = iota((8, 128), 0) < DEEP
    for pair in range(2):
        sides = []
        for group in (2 * pair, 2 * pair + 1):
            copies[2 * group].wait()
            copies[2 * group + 1].wait()
            total = None
            for component in range(3):
                real = f32(fwd[group, 0, component]) * f32(adj[group, 0, component])
                imag = f32(fwd[group, 1, component]) * f32(adj[group, 1, component])
                total = real - imag if total is None else total + (real - imag)
            sides.append((total * weight_ref[0]).reshape(128, 128))
        even, odd = (side.T.reshape(16, 8, 128) for side in sides)
        first = jnp.where(low, even, pltpu.roll(odd, DEEP, 1))
        second = jnp.where(low, pltpu.roll(even, DEEP, 1), odd)
        tiles = jnp.stack([first, second], axis=1).reshape(SLABS, 8, 128)
        terms_ref[:, 8 * pair : 8 * pair + 8, :] = tiles


def sensitivity(fwd, adj, weight):
    hbm = pl.BlockSpec(memory_space=pltpu.HBM)
    held = pltpu.VMEM((GROUPS, 2, 3, 8, 16, 128), jnp.bfloat16)
    return call(
        sensitivity_kernel,
        jax.ShapeDtypeStruct((SLABS, 16, 128), jnp.float32),
        in_specs=[hbm, hbm, pl.BlockSpec(memory_space=pltpu.SMEM)],
        out_specs=whole(1)[0],
        scratch_shapes=[held, held, pltpu.SemaphoreType.DMA((2 * GROUPS,))],
    )(in_hbm(fwd), in_hbm(adj), weight)


def middle_kernel(terms_ref, d_ref, m_ref, v_ref, out_ref, near_ref, far_ref):
    slab = lax.axis_index("illum")
    rows, cols = iota((8, 256), 0), iota((8, 256), 1)
    near = hat(slab * DEEP + (rows & 3), cols & 127)
    band = bf(jnp.where(((rows >> 2) & 1) == (cols >> 7), near, 0).astype(jnp.float32))
    own = []
    for pair in range(2):
        dens = d_ref[16 * pair : 16 * pair + 16].reshape(256, 128)
        dens = jnp.concatenate([dens[:128], dens[128:]], axis=1)
        own.append(sum(dot(band, part, ((1,), (1,))) for part in parts_of(dens, 2)))
    both = jnp.concatenate([jnp.sum(terms_ref[...], axis=0)] + own, axis=0)
    out_ref[...] = jnp.broadcast_to(both[None], out_ref.shape)
    near_at = pl.multiple_of(24 * (1 - (lax.axis_index("gx") & 1)), 8)
    for k, ref in enumerate((d_ref, m_ref, v_ref)):
        near_ref[k] = ref[pl.ds(near_at, 8)]
        far_ref[k] = ref[pl.ds(24 - near_at, 8)]


def middle(terms, density, moment_one, moment_two):
    edge = jax.ShapeDtypeStruct((3, 8, 16, 128), jnp.float32)
    return call(
        middle_kernel,
        (jax.ShapeDtypeStruct((16, 32, 128), jnp.float32), edge, edge),
        in_specs=whole(4),
        out_specs=tuple(whole(3)),
    )(terms, density, moment_one, moment_two)


def plane_taps():
    dx, dy, x, y = np.meshgrid(np.arange(-1, 2), np.arange(-1, 2), np.arange(8), np.arange(16), indexing="ij")
    far_x = (x + 8 * dx).reshape(-1, 1) - np.repeat(np.arange(8), 16)
    far_y = (y + 16 * dy).reshape(-1, 1) - np.tile(np.arange(16), 8)
    taps = np.maximum(TAPS - np.abs(far_x), 0) * np.maximum(TAPS - np.abs(far_y), 0)
    return jnp.asarray(taps.astype(np.float32)).astype(jnp.bfloat16)


PAD_X, PAD_Y = 3, 2


def slab_kernel(all_ref, taps_ref, out_ref, sens, dens):
    gx, gy = lax.axis_index("gx"), lax.axis_index("gy")
    low = iota((8, 128), 0) < DEEP
    zero = jnp.zeros((8, 128), jnp.float32)
    for ref in (sens, dens):
        for x in range(16 + 2 * PAD_X):
            for y in range(4 + 2 * PAD_Y):
                if not (PAD_X <= x < 16 + PAD_X and PAD_Y <= y < 4 + PAD_Y):
                    ref[x, y] = zero
    for x in range(4):
        for y in range(4):
            for pair in range(2):
                at = PAD_X + 4 * x + 2 * pair
                for ref, base in ((sens, 0), (dens, 16)):
                    tile = all_ref[4 * x + y, base + 8 * pair : base + 8 * pair + 8, :]
                    turned = pltpu.roll(tile, DEEP, 0)
                    twice = (jnp.where(low, tile, turned), jnp.where(low, turned, tile))
                    for odd in range(2):
                        value = twice[odd]
                        if base:
                            top = f32(bf(value))
                            value = jnp.where(low, top, value - top)
                        ref[at + odd, PAD_Y + y] = value
    taps = taps_ref[...]
    first = GROUPS * gx
    window = dens[pl.ds(first, 10), pl.ds(gy, 5)]
    side = jnp.concatenate(
        [bf(window[dx : dx + 8, dy : dy + 3].reshape(192, 128)) for dx in range(3) for dy in range(3)], axis=1
    )
    filtered = dot(side, taps, ((1,), (0,))).reshape(24, 8, 128)
    filtered = (filtered + pltpu.roll(filtered, DEEP, 1)) * (UNIT * UNIT * UNIT)
    inner = jnp.tanh(sharpness * (filtered - threshold))
    scale = jnp.tanh(jnp.full((8, 128), sharpness * threshold, jnp.float32)) * 2.0
    slope = sharpness * (1.0 - inner * inner) / scale
    chained = slope * sens[pl.ds(first + 1, 8), pl.ds(gy + 1, 3)].reshape(24, 8, 128)
    top = f32(bf(chained))
    chained = bf(jnp.where(low, top, chained - top)).reshape(8, 3, 8, 128)
    side = jnp.concatenate([chained[dx : dx + 6, dy].reshape(48, 128) for dx in range(3) for dy in range(3)], axis=1)
    result = dot(side, taps, ((1,), (0,))).reshape(6, 8, 128)
    result = result + pltpu.roll(result, DEEP, 1)
    for pair in range(3):
        tile = jnp.where(low, result[2 * pair], result[2 * pair + 1])
        out_ref[:, 8 * pair : 8 * pair + 8, :] = jnp.broadcast_to(tile[None], (SLABS, 8, 128))


def slab_step(everything):
    return call(
        slab_kernel,
        jax.ShapeDtypeStruct((SLABS, 24, 128), jnp.float32),
        in_specs=whole(2),
        out_specs=whole(1)[0],
        scratch_shapes=[pltpu.VMEM((16 + 2 * PAD_X, 4 + 2 * PAD_Y, 8, 128), jnp.float32)] * 2,
    )(everything, plane_taps())


def adam(density, moment_one, moment_two, gradient):
    new_one = 0.9 * moment_one + 0.1 * gradient
    new_two = 0.999 * moment_two + 0.001 * gradient * gradient
    first_fix = 1.0 - 0.9**5
    second_fix = 1.0 - 0.999**5
    step = new_one / first_fix / (jnp.sqrt(new_two / second_fix) + 1e-08)
    return jnp.clip(density - 0.05 * step, 0.0, 1.0), new_one, new_two


def box(value):
    n = value.shape[0]
    two = value[: n - 1] + value[1:]
    four = two[: n - 3] + two[2:]
    eight = four[: n - 7] + four[4:]
    return eight[: n - 8] + value[8:]


def adam_kernel(slabs_ref, d_ref, m_ref, v_ref, near_ref, far_ref, nd_ref, nm_ref, nv_ref, fx_ref, ynear_ref, yfar_ref, ext):
    gx, gy = lax.axis_index("gx"), lax.axis_index("gy")
    even_x, even_y = (gx & 1) == 0, (gy & 1) == 0
    rows, cols = iota((256, 256), 0), iota((256, 256), 1)
    depth = (rows >> 3) * DEEP + (rows & 3)
    near = jnp.where(((rows >> 2) & 1) == (cols >> 7), hat(depth, cols & 127), 0)
    band = bf(near.astype(jnp.float32))
    for pair in range(3):
        side = slabs_ref[:, 8 * pair : 8 * pair + 8, :].reshape(256, 128)
        both = sum(dot(part, band, ((0,), (0,))) for part in parts_of(side, 2)) * (UNIT * UNIT * UNIT)
        for odd in range(2):
            group = 2 * pair + odd - 1
            gradient = both[:, 128 * odd : 128 * odd + 128].reshape(8, 16, 128)
            if group == -1:
                left = [jnp.where(even_x, far_ref[k], near_ref[k]) for k in range(3)]
                new, _, _ = adam(*left, gradient)
                new = jnp.where(gx > 0, new, 0.0)
            elif group == GROUPS:
                right = [jnp.where(even_x, near_ref[k], far_ref[k]) for k in range(3)]
                new, _, _ = adam(*right, gradient)
                new = jnp.where(gx < lax.axis_size("gx") - 1, new, 0.0)
            else:
                at = slice(8 * group, 8 * group + 8)
                new, one, two = adam(d_ref[at], m_ref[at], v_ref[at], gradient)
                nd_ref[at] = new
                nm_ref[at] = one
                nv_ref[at] = two
            ext[8 * (group + 1) : 8 * (group + 1) + 8] = new
    along_x = box(box(ext[...])) * UNIT
    fx_ref[...] = along_x
    low, high = along_x[:, :8], along_x[:, 8:]
    ynear_ref[...] = jnp.where(even_y, high, low)
    yfar_ref[...] = jnp.where(even_y, low, high)


def adam_step(slabs, density, moment_one, moment_two, near, far):
    tile = jax.ShapeDtypeStruct((32, 16, 128), jnp.float32)
    half = jax.ShapeDtypeStruct((32, 8, 128), jnp.float32)
    return call(
        adam_kernel,
        (tile, tile, tile, tile, half, half),
        in_specs=whole(6),
        out_specs=tuple(whole(6)),
        scratch_shapes=[pltpu.VMEM((48, 16, 128), jnp.float32)],
    )(slabs, density, moment_one, moment_two, near, far)


def yz_filter(spread, sides):
    band = bf(hat(iota((128, 128), 0), iota((128, 128), 1)).astype(jnp.float32))
    side = jnp.concatenate(sides, axis=1)
    both = sum(dot(spread, part, ((1,), (0,))) for part in parts_of(side, 2))
    for odd in range(2):
        along_y = both[:, 128 * odd : 128 * odd + 128]
        yield sum(dot(part, band, ((1,), (0,))) for part in parts_of(along_y, 2)) * (UNIT * UNIT)


def own_kernel(fx_ref, nd_ref, nm_ref, nv_ref, own_ref, nd_out, nm_out, nv_out, sems):
    copies = [
        pltpu.make_async_copy(source, target, sems.at[k])
        for k, (source, target) in enumerate(((nd_ref, nd_out), (nm_ref, nm_out), (nv_ref, nv_out)))
    ]
    for copy in copies:
        copy.start()
    rows, cols = iota((128, 128), 0), iota((128, 128), 1)
    spread = bf(jnp.where((rows >> 4) == (cols >> 4), hat(rows & 15, cols & 15), 0).astype(jnp.float32))
    for pair in range(2):
        groups = [slice(8 * g, 8 * g + 8) for g in (2 * pair, 2 * pair + 1)]
        values = yz_filter(spread, [fx_ref[at].reshape(128, 128) for at in groups])
        for at, value in zip(groups, values):
            own_ref[at] = value.reshape(8, 16, 128)
    for copy in copies:
        copy.wait()


def own_step(along_x, *results):
    tile = jax.ShapeDtypeStruct((32, 16, 128), jnp.float32)
    return call(
        own_kernel,
        (tile, tile, tile, tile),
        in_specs=whole(4),
        out_specs=tuple(whole(1) + [pl.BlockSpec(memory_space=pltpu.HBM)] * 3),
        scratch_shapes=[pltpu.SemaphoreType.DMA((3,))],
    )(along_x, *results)


def physical_kernel(far_ref, own_ref, near_ref, out_ref, held, sems):
    even = (lax.axis_index("gy") & 1) == 0
    rows, cols = iota((128, 128), 0), iota((128, 128), 1)
    later = (cols < 64) == even
    y = (cols & 7) + jnp.where(later, 16, -8)
    spread = bf(jnp.where(((cols & 63) >> 3) == (rows >> 4), hat(y, rows & 15), 0).astype(jnp.float32))
    scale = jnp.tanh(jnp.full((128, 128), sharpness * threshold, jnp.float32))
    copies = []
    for pair in range(2):
        groups = [slice(8 * g, 8 * g + 8) for g in (2 * pair, 2 * pair + 1)]
        sides = [jnp.concatenate([near_ref[at].reshape(64, 128), far_ref[at].reshape(64, 128)], axis=0) for at in groups]
        for at, value in zip(groups, yz_filter(spread, sides)):
            value = value + own_ref[at].reshape(128, 128)
            value = (scale + jnp.tanh(sharpness * (value - threshold))) / (scale + scale)
            held[at] = value.reshape(8, 16, 128)
            copies.append(pltpu.make_async_copy(held.at[at], out_ref.at[at], sems.at[len(copies)]))
            copies[-1].start()
    for copy in copies:
        copy.wait()


def physical_step(own, near, far):
    return call(
        physical_kernel,
        jax.ShapeDtypeStruct((32, 16, 128), jnp.float32),
        in_specs=whole(3),
        out_specs=pl.BlockSpec(memory_space=pltpu.HBM),
        scratch_shapes=[pltpu.VMEM((32, 16, 128), jnp.float32), pltpu.SemaphoreType.DMA((GROUPS,))],
    )(far, own, near)


def swap(near, far, axis):
    size = lax.axis_size(axis)
    pairs = [(i, i ^ 1) for i in range(size)]
    others = [(i, j) for k in range(1, size - 1, 2) for i, j in ((k, k + 1), (k + 1, k))]
    far = lax.ppermute(far, axis, others)
    return lax.ppermute(near, axis, pairs), far


def exchange(value, axes):
    return lax.all_to_all(value, axes, 0, 0, tiled=True)


def shards(density, moment_one, moment_two, forward_field, adjoint_field, objective_weight):
    state = (density, moment_one, moment_two)
    terms = exchange(sensitivity(forward_field, adjoint_field, objective_weight), "illum")
    both, near, far = middle(terms, *state)
    slab = slab_step(exchange(both, ("gx", "gy")))
    slab, near, far = lax.optimization_barrier((slab, near, far))
    slabs = exchange(slab, "illum")
    near, far = swap(near, far, "gx")
    *results, along_x, near, far = adam_step(slabs, *state, near, far)
    near, far = swap(near, far, "gy")
    own, *results = own_step(along_x, *results)
    return (*results, physical_step(own, near, far))


def solution(mesh):
    tile = P("gx", "gy", None)
    field = P("illum", None, None, "gx", "gy", None)
    return jax.shard_map(
        shards,
        mesh=mesh,
        in_specs=(tile, tile, tile, field, field, P("illum")),
        out_specs=(tile, tile, tile, tile),
        check_vma=False,
    )
```

```python
import jax
import jax.numpy as jnp
import numpy as np
from jax import lax
from jax.experimental import pallas as pl
from jax.experimental.pallas import tpu as pltpu
from jax.sharding import PartitionSpec as P

RADIUS = 8
TAPS = RADIUS + 1
UNIT = 1.0 / float(TAPS**2)
sharpness = 8.0
threshold = 0.5

GROUPS = 4
SLABS = 32
DEEP = 4


def call(kernel, out_shape, limit=48 * 1024 * 1024, **more):
    return pl.pallas_call(
        kernel,
        out_shape=out_shape,
        compiler_params=pltpu.CompilerParams(vmem_limit_bytes=limit),
        **more,
    )


def in_hbm(value):
    return pltpu.with_memory_space_constraint(value, pltpu.HBM)


def whole(count):
    return [pl.BlockSpec(memory_space=pltpu.VMEM)] * count


def hat(a, b):
    return jnp.maximum(TAPS - jnp.abs(a - b), 0)


def bf(value):
    return value.astype(jnp.bfloat16)


def f32(value):
    return value.astype(jnp.float32)


def parts_of(value, count):
    out = []
    for _ in range(count):
        part = bf(value)
        out.append(part)
        value = value - f32(part)
    return out


def dot(a, b, dims):
    return lax.dot_general(a, b, (dims, ((), ())), preferred_element_type=jnp.float32)


def iota(shape, dim):
    return lax.broadcasted_iota(jnp.int32, shape, dim)


def sensitivity_kernel(fwd_ref, adj_ref, weight_ref, terms_ref, fwd, adj, sems):
    copies = []
    for group in range(GROUPS):
        for which, (source, target) in enumerate(((fwd_ref, fwd), (adj_ref, adj))):
            piece = source.at[0, :, :, pl.ds(8 * group, 8)]
            copies.append(pltpu.make_async_copy(piece, target.at[group], sems.at[2 * group + which]))
            copies[-1].start()
    low = iota((8, 128), 0) < DEEP
    for pair in range(2):
        sides = []
        for group in (2 * pair, 2 * pair + 1):
            copies[2 * group].wait()
            copies[2 * group + 1].wait()
            total = None
            for component in range(3):
                real = f32(fwd[group, 0, component]) * f32(adj[group, 0, component])
                imag = f32(fwd[group, 1, component]) * f32(adj[group, 1, component])
                total = real - imag if total is None else total + (real - imag)
            sides.append((total * weight_ref[0]).reshape(128, 128))
        even, odd = (side.T.reshape(16, 8, 128) for side in sides)
        first = jnp.where(low, even, pltpu.roll(odd, DEEP, 1))
        second = jnp.where(low, pltpu.roll(even, DEEP, 1), odd)
        tiles = jnp.stack([first, second], axis=1).reshape(SLABS, 8, 128)
        terms_ref[:, 8 * pair : 8 * pair + 8, :] = tiles


def sensitivity(fwd, adj, weight):
    hbm = pl.BlockSpec(memory_space=pltpu.HBM)
    held = pltpu.VMEM((GROUPS, 2, 3, 8, 16, 128), jnp.bfloat16)
    return call(
        sensitivity_kernel,
        jax.ShapeDtypeStruct((SLABS, 16, 128), jnp.float32),
        in_specs=[hbm, hbm, pl.BlockSpec(memory_space=pltpu.SMEM)],
        out_specs=whole(1)[0],
        scratch_shapes=[held, held, pltpu.SemaphoreType.DMA((2 * GROUPS,))],
    )(in_hbm(fwd), in_hbm(adj), weight)


def middle_kernel(terms_ref, d_ref, m_ref, v_ref, out_ref, near_ref, far_ref):
    slab = SLABS - 1 - lax.axis_index("illum")
    rows, cols = iota((8, 256), 0), iota((8, 256), 1)
    near = hat(slab * DEEP + (rows & 3), cols & 127)
    band = bf(jnp.where(((rows >> 2) & 1) == (cols >> 7), near, 0).astype(jnp.float32))
    own = []
    for pair in range(2):
        dens = d_ref[16 * pair : 16 * pair + 16].reshape(256, 128)
        dens = jnp.concatenate([dens[:128], dens[128:]], axis=1)
        own.append(sum(dot(band, part, ((1,), (1,))) for part in parts_of(dens, 2)))
    both = jnp.concatenate([jnp.sum(terms_ref[...], axis=0)] + own, axis=0)
    out_ref[...] = jnp.broadcast_to(both[None], out_ref.shape)
    near_at = pl.multiple_of(24 * (1 - (lax.axis_index("gx") & 1)), 8)
    for k, ref in enumerate((d_ref, m_ref, v_ref)):
        near_ref[k] = ref[pl.ds(near_at, 8)]
        far_ref[k] = ref[pl.ds(24 - near_at, 8)]


def middle(terms, density, moment_one, moment_two):
    edge = jax.ShapeDtypeStruct((3, 8, 16, 128), jnp.float32)
    return call(
        middle_kernel,
        (jax.ShapeDtypeStruct((16, 32, 128), jnp.float32), edge, edge),
        in_specs=whole(4),
        out_specs=tuple(whole(3)),
    )(terms, density, moment_one, moment_two)


def plane_taps():
    dx, dy, x, y = np.meshgrid(np.arange(-1, 2), np.arange(-1, 2), np.arange(8), np.arange(16), indexing="ij")
    far_x = (x + 8 * dx).reshape(-1, 1) - np.repeat(np.arange(8), 16)
    far_y = (y + 16 * dy).reshape(-1, 1) - np.tile(np.arange(16), 8)
    taps = np.maximum(TAPS - np.abs(far_x), 0) * np.maximum(TAPS - np.abs(far_y), 0)
    return jnp.asarray(taps.astype(np.float32)).astype(jnp.bfloat16)


PAD_X, PAD_Y = 3, 2


def slab_kernel(all_ref, taps_ref, out_ref, sens, dens):
    gx, gy = lax.axis_index("gx"), lax.axis_index("gy")
    low = iota((8, 128), 0) < DEEP
    zero = jnp.zeros((8, 128), jnp.float32)
    for ref in (sens, dens):
        for x in range(16 + 2 * PAD_X):
            for y in range(4 + 2 * PAD_Y):
                if not (PAD_X <= x < 16 + PAD_X and PAD_Y <= y < 4 + PAD_Y):
                    ref[x, y] = zero
    for x in range(4):
        for y in range(4):
            for pair in range(2):
                at = PAD_X + 4 * x + 2 * pair
                for ref, base in ((sens, 0), (dens, 16)):
                    tile = all_ref[4 * x + y, base + 8 * pair : base + 8 * pair + 8, :]
                    turned = pltpu.roll(tile, DEEP, 0)
                    twice = (jnp.where(low, tile, turned), jnp.where(low, turned, tile))
                    for odd in range(2):
                        value = twice[odd]
                        if base:
                            top = f32(bf(value))
                            value = jnp.where(low, top, value - top)
                        ref[at + odd, PAD_Y + y] = value
    taps = taps_ref[...]
    first = GROUPS * gx
    window = dens[pl.ds(first, 10), pl.ds(gy, 5)]
    side = jnp.concatenate(
        [bf(window[dx : dx + 8, dy : dy + 3].reshape(192, 128)) for dx in range(3) for dy in range(3)], axis=1
    )
    filtered = dot(side, taps, ((1,), (0,))).reshape(24, 8, 128)
    filtered = (filtered + pltpu.roll(filtered, DEEP, 1)) * (UNIT * UNIT * UNIT)
    inner = jnp.tanh(sharpness * (filtered - threshold))
    scale = jnp.tanh(jnp.full((8, 128), sharpness * threshold, jnp.float32)) * 2.0
    slope = sharpness * (1.0 - inner * inner) / scale
    chained = slope * sens[pl.ds(first + 1, 8), pl.ds(gy + 1, 3)].reshape(24, 8, 128)
    top = f32(bf(chained))
    chained = bf(jnp.where(low, top, chained - top)).reshape(8, 3, 8, 128)
    side = jnp.concatenate([chained[dx : dx + 6, dy].reshape(48, 128) for dx in range(3) for dy in range(3)], axis=1)
    result = dot(side, taps, ((1,), (0,))).reshape(6, 8, 128)
    result = result + pltpu.roll(result, DEEP, 1)
    for pair in range(3):
        tile = jnp.where(low, result[2 * pair], result[2 * pair + 1])
        out_ref[:, 8 * pair : 8 * pair + 8, :] = jnp.broadcast_to(tile[None], (SLABS, 8, 128))


def slab_step(everything):
    return call(
        slab_kernel,
        jax.ShapeDtypeStruct((SLABS, 24, 128), jnp.float32),
        in_specs=whole(2),
        out_specs=whole(1)[0],
        scratch_shapes=[pltpu.VMEM((16 + 2 * PAD_X, 4 + 2 * PAD_Y, 8, 128), jnp.float32)] * 2,
    )(everything, plane_taps())


def adam(density, moment_one, moment_two, gradient):
    new_one = 0.9 * moment_one + 0.1 * gradient
    new_two = 0.999 * moment_two + 0.001 * gradient * gradient
    first_fix = 1.0 - 0.9**5
    second_fix = 1.0 - 0.999**5
    step = new_one / first_fix / (jnp.sqrt(new_two / second_fix) + 1e-08)
    return jnp.clip(density - 0.05 * step, 0.0, 1.0), new_one, new_two


def box(value):
    n = value.shape[0]
    two = value[: n - 1] + value[1:]
    four = two[: n - 3] + two[2:]
    eight = four[: n - 7] + four[4:]
    return eight[: n - 8] + value[8:]


def adam_kernel(slabs_ref, d_ref, m_ref, v_ref, near_ref, far_ref, nd_ref, nm_ref, nv_ref, fx_ref, ynear_ref, yfar_ref, ext):
    gx, gy = lax.axis_index("gx"), lax.axis_index("gy")
    even_x, even_y = (gx & 1) == 0, (gy & 1) == 0
    rows, cols = iota((256, 256), 0), iota((256, 256), 1)
    depth = (rows >> 3) * DEEP + (rows & 3)
    near = jnp.where(((rows >> 2) & 1) == (cols >> 7), hat(depth, cols & 127), 0)
    band = bf(near.astype(jnp.float32))
    for pair in range(3):
        side = slabs_ref[:, 8 * pair : 8 * pair + 8, :].reshape(256, 128)
        both = sum(dot(part, band, ((0,), (0,))) for part in parts_of(side, 2)) * (UNIT * UNIT * UNIT)
        for odd in range(2):
            group = 2 * pair + odd - 1
            gradient = both[:, 128 * odd : 128 * odd + 128].reshape(8, 16, 128)
            if group == -1:
                left = [jnp.where(even_x, far_ref[k], near_ref[k]) for k in range(3)]
                new, _, _ = adam(*left, gradient)
                new = jnp.where(gx > 0, new, 0.0)
            elif group == GROUPS:
                right = [jnp.where(even_x, near_ref[k], far_ref[k]) for k in range(3)]
                new, _, _ = adam(*right, gradient)
                new = jnp.where(gx < lax.axis_size("gx") - 1, new, 0.0)
            else:
                at = slice(8 * group, 8 * group + 8)
                new, one, two = adam(d_ref[at], m_ref[at], v_ref[at], gradient)
                nd_ref[at] = new
                nm_ref[at] = one
                nv_ref[at] = two
            ext[8 * (group + 1) : 8 * (group + 1) + 8] = new
    along_x = box(box(ext[...])) * UNIT
    fx_ref[...] = along_x
    low, high = along_x[:, :8], along_x[:, 8:]
    ynear_ref[...] = jnp.where(even_y, high, low)
    yfar_ref[...] = jnp.where(even_y, low, high)


def adam_step(slabs, density, moment_one, moment_two, near, far):
    tile = jax.ShapeDtypeStruct((32, 16, 128), jnp.float32)
    half = jax.ShapeDtypeStruct((32, 8, 128), jnp.float32)
    return call(
        adam_kernel,
        (tile, tile, tile, tile, half, half),
        in_specs=whole(6),
        out_specs=tuple(whole(6)),
        scratch_shapes=[pltpu.VMEM((48, 16, 128), jnp.float32)],
    )(slabs, density, moment_one, moment_two, near, far)


def yz_filter(spread, sides):
    band = bf(hat(iota((128, 128), 0), iota((128, 128), 1)).astype(jnp.float32))
    side = jnp.concatenate(sides, axis=1)
    both = sum(dot(spread, part, ((1,), (0,))) for part in parts_of(side, 2))
    for odd in range(2):
        along_y = both[:, 128 * odd : 128 * odd + 128]
        yield sum(dot(part, band, ((1,), (0,))) for part in parts_of(along_y, 2)) * (UNIT * UNIT)


def own_kernel(fx_ref, nd_ref, nm_ref, nv_ref, own_ref, nd_out, nm_out, nv_out, sems):
    copies = [
        pltpu.make_async_copy(source, target, sems.at[k])
        for k, (source, target) in enumerate(((nd_ref, nd_out), (nm_ref, nm_out), (nv_ref, nv_out)))
    ]
    for copy in copies:
        copy.start()
    rows, cols = iota((128, 128), 0), iota((128, 128), 1)
    spread = bf(jnp.where((rows >> 4) == (cols >> 4), hat(rows & 15, cols & 15), 0).astype(jnp.float32))
    for pair in range(2):
        groups = [slice(8 * g, 8 * g + 8) for g in (2 * pair, 2 * pair + 1)]
        values = yz_filter(spread, [fx_ref[at].reshape(128, 128) for at in groups])
        for at, value in zip(groups, values):
            own_ref[at] = value.reshape(8, 16, 128)
    for copy in copies:
        copy.wait()


def own_step(along_x, *results):
    tile = jax.ShapeDtypeStruct((32, 16, 128), jnp.float32)
    return call(
        own_kernel,
        (tile, tile, tile, tile),
        in_specs=whole(4),
        out_specs=tuple(whole(1) + [pl.BlockSpec(memory_space=pltpu.HBM)] * 3),
        scratch_shapes=[pltpu.SemaphoreType.DMA((3,))],
    )(along_x, *results)


def physical_kernel(far_ref, own_ref, near_ref, out_ref, held, sems):
    even = (lax.axis_index("gy") & 1) == 0
    rows, cols = iota((128, 128), 0), iota((128, 128), 1)
    later = (cols < 64) == even
    y = (cols & 7) + jnp.where(later, 16, -8)
    spread = bf(jnp.where(((cols & 63) >> 3) == (rows >> 4), hat(y, rows & 15), 0).astype(jnp.float32))
    scale = jnp.tanh(jnp.full((128, 128), sharpness * threshold, jnp.float32))
    copies = []
    for pair in range(2):
        groups = [slice(8 * g, 8 * g + 8) for g in (2 * pair, 2 * pair + 1)]
        sides = [jnp.concatenate([near_ref[at].reshape(64, 128), far_ref[at].reshape(64, 128)], axis=0) for at in groups]
        for at, value in zip(groups, yz_filter(spread, sides)):
            value = value + own_ref[at].reshape(128, 128)
            value = (scale + jnp.tanh(sharpness * (value - threshold))) / (scale + scale)
            held[at] = value.reshape(8, 16, 128)
            copies.append(pltpu.make_async_copy(held.at[at], out_ref.at[at], sems.at[len(copies)]))
            copies[-1].start()
    for copy in copies:
        copy.wait()


def physical_step(own, near, far):
    return call(
        physical_kernel,
        jax.ShapeDtypeStruct((32, 16, 128), jnp.float32),
        in_specs=whole(3),
        out_specs=pl.BlockSpec(memory_space=pltpu.HBM),
        scratch_shapes=[pltpu.VMEM((32, 16, 128), jnp.float32), pltpu.SemaphoreType.DMA((GROUPS,))],
    )(far, own, near)


def swap(near, far, axis):
    size = lax.axis_size(axis)
    pairs = [(i, i ^ 1) for i in range(size)]
    others = [(i, j) for k in range(1, size - 1, 2) for i, j in ((k, k + 1), (k + 1, k))]
    far = lax.ppermute(far, axis, others)
    return lax.ppermute(near, axis, pairs), far


def exchange(value, axes, groups=None):
    return lax.all_to_all(value, axes, 0, 0, tiled=True, axis_index_groups=groups)


def countdown(axis):
    return [list(reversed(range(lax.axis_size(axis))))]


def shards(density, moment_one, moment_two, forward_field, adjoint_field, objective_weight):
    state = (density, moment_one, moment_two)
    terms = exchange(sensitivity(forward_field, adjoint_field, objective_weight), "illum", countdown("illum"))
    both, near, far = middle(terms, *state)
    slab = slab_step(exchange(both, ("gx", "gy")))
    slab, near, far = lax.optimization_barrier((slab, near, far))
    slabs = exchange(slab, "illum", countdown("illum"))
    near, far = swap(near, far, "gx")
    *results, along_x, near, far = adam_step(slabs, *state, near, far)
    near, far = swap(near, far, "gy")
    own, *results = own_step(along_x, *results)
    return (*results, physical_step(own, near, far))


def solution(mesh):
    tile = P("gx", "gy", None)
    field = P("illum", None, None, "gx", "gy", None)
    return jax.shard_map(
        shards,
        mesh=mesh,
        in_specs=(tile, tile, tile, field, field, P("illum")),
        out_specs=(tile, tile, tile, tile),
        check_vma=False,
    )
```

```python
import jax
import jax.numpy as jnp
import numpy as np
from jax import lax
from jax.experimental import pallas as pl
from jax.experimental.pallas import tpu as pltpu
from jax.sharding import PartitionSpec as P

RADIUS = 8
TAPS = RADIUS + 1
UNIT = 1.0 / float(TAPS**2)
sharpness = 8.0
threshold = 0.5

GROUPS = 4
SLABS = 32
DEEP = 4


def call(kernel, out_shape, limit=48 * 1024 * 1024, **more):
    return pl.pallas_call(
        kernel,
        out_shape=out_shape,
        compiler_params=pltpu.CompilerParams(vmem_limit_bytes=limit),
        **more,
    )


def in_hbm(value):
    return pltpu.with_memory_space_constraint(value, pltpu.HBM)


def whole(count):
    return [pl.BlockSpec(memory_space=pltpu.VMEM)] * count


def hat(a, b):
    return jnp.maximum(TAPS - jnp.abs(a - b), 0)


def bf(value):
    return value.astype(jnp.bfloat16)


def f32(value):
    return value.astype(jnp.float32)


def parts_of(value, count):
    out = []
    for _ in range(count):
        part = bf(value)
        out.append(part)
        value = value - f32(part)
    return out


def dot(a, b, dims):
    return lax.dot_general(a, b, (dims, ((), ())), preferred_element_type=jnp.float32)


def iota(shape, dim):
    return lax.broadcasted_iota(jnp.int32, shape, dim)


def sensitivity_kernel(fwd_ref, adj_ref, weight_ref, terms_ref, fwd, adj, sems):
    copies = []
    for group in range(GROUPS):
        for which, (source, target) in enumerate(((fwd_ref, fwd), (adj_ref, adj))):
            piece = source.at[0, :, :, pl.ds(8 * group, 8)]
            copies.append(pltpu.make_async_copy(piece, target.at[group], sems.at[2 * group + which]))
            copies[-1].start()
    low = iota((8, 128), 0) < DEEP
    for pair in range(2):
        sides = []
        for group in (2 * pair, 2 * pair + 1):
            copies[2 * group].wait()
            copies[2 * group + 1].wait()
            total = None
            for component in range(3):
                real = f32(fwd[group, 0, component]) * f32(adj[group, 0, component])
                imag = f32(fwd[group, 1, component]) * f32(adj[group, 1, component])
                total = real - imag if total is None else total + (real - imag)
            sides.append((total * weight_ref[0]).reshape(128, 128))
        even, odd = (side.T.reshape(16, 8, 128) for side in sides)
        first = jnp.where(low, even, pltpu.roll(odd, DEEP, 1))
        second = jnp.where(low, pltpu.roll(even, DEEP, 1), odd)
        tiles = jnp.stack([first, second], axis=1).reshape(SLABS, 8, 128)
        terms_ref[:, 8 * pair : 8 * pair + 8, :] = tiles


def sensitivity(fwd, adj, weight):
    hbm = pl.BlockSpec(memory_space=pltpu.HBM)
    held = pltpu.VMEM((GROUPS, 2, 3, 8, 16, 128), jnp.bfloat16)
    return call(
        sensitivity_kernel,
        jax.ShapeDtypeStruct((SLABS, 16, 128), jnp.float32),
        in_specs=[hbm, hbm, pl.BlockSpec(memory_space=pltpu.SMEM)],
        out_specs=whole(1)[0],
        scratch_shapes=[held, held, pltpu.SemaphoreType.DMA((2 * GROUPS,))],
    )(in_hbm(fwd), in_hbm(adj), weight)


def middle_kernel(terms_ref, d_ref, m_ref, v_ref, out_ref, near_ref, far_ref):
    slab = SLABS - 1 - lax.axis_index("illum")
    rows, cols = iota((8, 256), 0), iota((8, 256), 1)
    near = hat(slab * DEEP + (rows & 3), cols & 127)
    band = bf(jnp.where(((rows >> 2) & 1) == (cols >> 7), near, 0).astype(jnp.float32))
    own = []
    for pair in range(2):
        dens = d_ref[16 * pair : 16 * pair + 16].reshape(256, 128)
        dens = jnp.concatenate([dens[:128], dens[128:]], axis=1)
        own.append(sum(dot(band, part, ((1,), (1,))) for part in parts_of(dens, 2)))
    both = jnp.concatenate([jnp.sum(terms_ref[...], axis=0)] + own, axis=0)
    out_ref[...] = jnp.broadcast_to(both[None], out_ref.shape)
    near_at = pl.multiple_of(24 * (1 - (lax.axis_index("gx") & 1)), 8)
    for k, ref in enumerate((d_ref, m_ref, v_ref)):
        near_ref[k] = ref[pl.ds(near_at, 8)]
        far_ref[k] = ref[pl.ds(24 - near_at, 8)]


def middle(terms, density, moment_one, moment_two):
    edge = jax.ShapeDtypeStruct((3, 8, 16, 128), jnp.float32)
    return call(
        middle_kernel,
        (jax.ShapeDtypeStruct((16, 32, 128), jnp.float32), edge, edge),
        in_specs=whole(4),
        out_specs=tuple(whole(3)),
    )(terms, density, moment_one, moment_two)


def plane_taps():
    dx, dy, x, y = np.meshgrid(np.arange(-1, 2), np.arange(-1, 2), np.arange(8), np.arange(16), indexing="ij")
    far_x = (x + 8 * dx).reshape(-1, 1) - np.repeat(np.arange(8), 16)
    far_y = (y + 16 * dy).reshape(-1, 1) - np.tile(np.arange(16), 8)
    taps = np.maximum(TAPS - np.abs(far_x), 0) * np.maximum(TAPS - np.abs(far_y), 0)
    return jnp.asarray(taps.astype(np.float32)).astype(jnp.bfloat16)


PAD_X, PAD_Y = 3, 2


def slab_kernel(all_ref, taps_ref, out_ref, sens, dens):
    gx, gy = lax.axis_index("gx"), lax.axis_index("gy")
    low = iota((8, 128), 0) < DEEP
    zero = jnp.zeros((8, 128), jnp.float32)
    for ref in (sens, dens):
        for x in range(16 + 2 * PAD_X):
            for y in range(4 + 2 * PAD_Y):
                if not (PAD_X <= x < 16 + PAD_X and PAD_Y <= y < 4 + PAD_Y):
                    ref[x, y] = zero
    for x in range(4):
        for y in range(4):
            for pair in range(2):
                at = PAD_X + 4 * x + 2 * pair
                for ref, base in ((sens, 0), (dens, 16)):
                    tile = all_ref[15 - (4 * x + y), base + 8 * pair : base + 8 * pair + 8, :]
                    turned = pltpu.roll(tile, DEEP, 0)
                    twice = (jnp.where(low, tile, turned), jnp.where(low, turned, tile))
                    for odd in range(2):
                        value = twice[odd]
                        if base:
                            top = f32(bf(value))
                            value = jnp.where(low, top, value - top)
                        ref[at + odd, PAD_Y + y] = value
    taps = taps_ref[...]
    first = GROUPS * gx
    window = dens[pl.ds(first, 10), pl.ds(gy, 5)]
    side = jnp.concatenate(
        [bf(window[dx : dx + 8, dy : dy + 3].reshape(192, 128)) for dx in range(3) for dy in range(3)], axis=1
    )
    filtered = dot(side, taps, ((1,), (0,))).reshape(24, 8, 128)
    filtered = (filtered + pltpu.roll(filtered, DEEP, 1)) * (UNIT * UNIT * UNIT)
    inner = jnp.tanh(sharpness * (filtered - threshold))
    scale = jnp.tanh(jnp.full((8, 128), sharpness * threshold, jnp.float32)) * 2.0
    slope = sharpness * (1.0 - inner * inner) / scale
    chained = slope * sens[pl.ds(first + 1, 8), pl.ds(gy + 1, 3)].reshape(24, 8, 128)
    top = f32(bf(chained))
    chained = bf(jnp.where(low, top, chained - top)).reshape(8, 3, 8, 128)
    side = jnp.concatenate([chained[dx : dx + 6, dy].reshape(48, 128) for dx in range(3) for dy in range(3)], axis=1)
    result = dot(side, taps, ((1,), (0,))).reshape(6, 8, 128)
    result = result + pltpu.roll(result, DEEP, 1)
    for pair in range(3):
        tile = jnp.where(low, result[2 * pair], result[2 * pair + 1])
        out_ref[:, 8 * pair : 8 * pair + 8, :] = jnp.broadcast_to(tile[None], (SLABS, 8, 128))


def slab_step(everything):
    return call(
        slab_kernel,
        jax.ShapeDtypeStruct((SLABS, 24, 128), jnp.float32),
        in_specs=whole(2),
        out_specs=whole(1)[0],
        scratch_shapes=[pltpu.VMEM((16 + 2 * PAD_X, 4 + 2 * PAD_Y, 8, 128), jnp.float32)] * 2,
    )(everything, plane_taps())


def adam(density, moment_one, moment_two, gradient):
    new_one = 0.9 * moment_one + 0.1 * gradient
    new_two = 0.999 * moment_two + 0.001 * gradient * gradient
    first_fix = 1.0 - 0.9**5
    second_fix = 1.0 - 0.999**5
    step = new_one / first_fix / (jnp.sqrt(new_two / second_fix) + 1e-08)
    return jnp.clip(density - 0.05 * step, 0.0, 1.0), new_one, new_two


def box(value):
    n = value.shape[0]
    two = value[: n - 1] + value[1:]
    four = two[: n - 3] + two[2:]
    eight = four[: n - 7] + four[4:]
    return eight[: n - 8] + value[8:]


def adam_kernel(slabs_ref, d_ref, m_ref, v_ref, near_ref, far_ref, nd_ref, nm_ref, nv_ref, fx_ref, ynear_ref, yfar_ref, ext):
    gx, gy = lax.axis_index("gx"), lax.axis_index("gy")
    even_x, even_y = (gx & 1) == 0, (gy & 1) == 0
    rows, cols = iota((256, 256), 0), iota((256, 256), 1)
    depth = (rows >> 3) * DEEP + (rows & 3)
    near = jnp.where(((rows >> 2) & 1) == (cols >> 7), hat(depth, cols & 127), 0)
    band = bf(near.astype(jnp.float32))
    for pair in range(3):
        side = slabs_ref[:, 8 * pair : 8 * pair + 8, :].reshape(256, 128)
        both = sum(dot(part, band, ((0,), (0,))) for part in parts_of(side, 2)) * (UNIT * UNIT * UNIT)
        for odd in range(2):
            group = 2 * pair + odd - 1
            gradient = both[:, 128 * odd : 128 * odd + 128].reshape(8, 16, 128)
            if group == -1:
                left = [jnp.where(even_x, far_ref[k], near_ref[k]) for k in range(3)]
                new, _, _ = adam(*left, gradient)
                new = jnp.where(gx > 0, new, 0.0)
            elif group == GROUPS:
                right = [jnp.where(even_x, near_ref[k], far_ref[k]) for k in range(3)]
                new, _, _ = adam(*right, gradient)
                new = jnp.where(gx < lax.axis_size("gx") - 1, new, 0.0)
            else:
                at = slice(8 * group, 8 * group + 8)
                new, one, two = adam(d_ref[at], m_ref[at], v_ref[at], gradient)
                nd_ref[at] = new
                nm_ref[at] = one
                nv_ref[at] = two
            ext[8 * (group + 1) : 8 * (group + 1) + 8] = new
    along_x = box(box(ext[...])) * UNIT
    fx_ref[...] = along_x
    low, high = along_x[:, :8], along_x[:, 8:]
    ynear_ref[...] = jnp.where(even_y, high, low)
    yfar_ref[...] = jnp.where(even_y, low, high)


def adam_step(slabs, density, moment_one, moment_two, near, far):
    tile = jax.ShapeDtypeStruct((32, 16, 128), jnp.float32)
    half = jax.ShapeDtypeStruct((32, 8, 128), jnp.float32)
    return call(
        adam_kernel,
        (tile, tile, tile, tile, half, half),
        in_specs=whole(6),
        out_specs=tuple(whole(6)),
        scratch_shapes=[pltpu.VMEM((48, 16, 128), jnp.float32)],
    )(slabs, density, moment_one, moment_two, near, far)


def yz_filter(spread, sides):
    band = bf(hat(iota((128, 128), 0), iota((128, 128), 1)).astype(jnp.float32))
    side = jnp.concatenate(sides, axis=1)
    both = sum(dot(spread, part, ((1,), (0,))) for part in parts_of(side, 2))
    for odd in range(2):
        along_y = both[:, 128 * odd : 128 * odd + 128]
        yield sum(dot(part, band, ((1,), (0,))) for part in parts_of(along_y, 2)) * (UNIT * UNIT)


def own_kernel(fx_ref, nd_ref, nm_ref, nv_ref, own_ref, nd_out, nm_out, nv_out, sems):
    copies = [
        pltpu.make_async_copy(source, target, sems.at[k])
        for k, (source, target) in enumerate(((nd_ref, nd_out), (nm_ref, nm_out), (nv_ref, nv_out)))
    ]
    for copy in copies:
        copy.start()
    rows, cols = iota((128, 128), 0), iota((128, 128), 1)
    spread = bf(jnp.where((rows >> 4) == (cols >> 4), hat(rows & 15, cols & 15), 0).astype(jnp.float32))
    for pair in range(2):
        groups = [slice(8 * g, 8 * g + 8) for g in (2 * pair, 2 * pair + 1)]
        values = yz_filter(spread, [fx_ref[at].reshape(128, 128) for at in groups])
        for at, value in zip(groups, values):
            own_ref[at] = value.reshape(8, 16, 128)
    for copy in copies:
        copy.wait()


def own_step(along_x, *results):
    tile = jax.ShapeDtypeStruct((32, 16, 128), jnp.float32)
    return call(
        own_kernel,
        (tile, tile, tile, tile),
        in_specs=whole(4),
        out_specs=tuple(whole(1) + [pl.BlockSpec(memory_space=pltpu.HBM)] * 3),
        scratch_shapes=[pltpu.SemaphoreType.DMA((3,))],
    )(along_x, *results)


def physical_kernel(far_ref, own_ref, near_ref, out_ref, held, sems):
    even = (lax.axis_index("gy") & 1) == 0
    rows, cols = iota((128, 128), 0), iota((128, 128), 1)
    later = (cols < 64) == even
    y = (cols & 7) + jnp.where(later, 16, -8)
    spread = bf(jnp.where(((cols & 63) >> 3) == (rows >> 4), hat(y, rows & 15), 0).astype(jnp.float32))
    scale = jnp.tanh(jnp.full((128, 128), sharpness * threshold, jnp.float32))
    copies = []
    for pair in range(2):
        groups = [slice(8 * g, 8 * g + 8) for g in (2 * pair, 2 * pair + 1)]
        sides = [jnp.concatenate([near_ref[at].reshape(64, 128), far_ref[at].reshape(64, 128)], axis=0) for at in groups]
        for at, value in zip(groups, yz_filter(spread, sides)):
            value = value + own_ref[at].reshape(128, 128)
            value = (scale + jnp.tanh(sharpness * (value - threshold))) / (scale + scale)
            held[at] = value.reshape(8, 16, 128)
            copies.append(pltpu.make_async_copy(held.at[at], out_ref.at[at], sems.at[len(copies)]))
            copies[-1].start()
    for copy in copies:
        copy.wait()


def physical_step(own, near, far):
    return call(
        physical_kernel,
        jax.ShapeDtypeStruct((32, 16, 128), jnp.float32),
        in_specs=whole(3),
        out_specs=pl.BlockSpec(memory_space=pltpu.HBM),
        scratch_shapes=[pltpu.VMEM((32, 16, 128), jnp.float32), pltpu.SemaphoreType.DMA((GROUPS,))],
    )(far, own, near)


def swap(near, far, axis):
    size = lax.axis_size(axis)
    pairs = [(i, i ^ 1) for i in range(size)]
    others = [(i, j) for k in range(1, size - 1, 2) for i, j in ((k, k + 1), (k + 1, k))]
    far = lax.ppermute(far, axis, others)
    return lax.ppermute(near, axis, pairs), far


def exchange(value, axes, groups=None):
    return lax.all_to_all(value, axes, 0, 0, tiled=True, axis_index_groups=groups)


def countdown(axes):
    return [list(reversed(range(lax.axis_size(axes))))]


def shards(density, moment_one, moment_two, forward_field, adjoint_field, objective_weight):
    state = (density, moment_one, moment_two)
    terms = exchange(sensitivity(forward_field, adjoint_field, objective_weight), "illum", countdown("illum"))
    both, near, far = middle(terms, *state)
    slab = slab_step(exchange(both, ("gx", "gy"), countdown(("gx", "gy"))))
    slab, near, far = lax.optimization_barrier((slab, near, far))
    slabs = exchange(slab, "illum", countdown("illum"))
    near, far = swap(near, far, "gx")
    *results, along_x, near, far = adam_step(slabs, *state, near, far)
    near, far = swap(near, far, "gy")
    own, *results = own_step(along_x, *results)
    return (*results, physical_step(own, near, far))


def solution(mesh):
    tile = P("gx", "gy", None)
    field = P("illum", None, None, "gx", "gy", None)
    return jax.shard_map(
        shards,
        mesh=mesh,
        in_specs=(tile, tile, tile, field, field, P("illum")),
        out_specs=(tile, tile, tile, tile),
        check_vma=False,
    )
```

```python
import jax
import jax.numpy as jnp
import numpy as np
from jax import lax
from jax.experimental import pallas as pl
from jax.experimental.pallas import tpu as pltpu
from jax.sharding import PartitionSpec as P

RADIUS = 8
TAPS = RADIUS + 1
UNIT = 1.0 / float(TAPS**2)
sharpness = 8.0
threshold = 0.5

GROUPS = 4
SLABS = 32
DEEP = 4


def call(kernel, out_shape, limit=48 * 1024 * 1024, **more):
    return pl.pallas_call(
        kernel,
        out_shape=out_shape,
        compiler_params=pltpu.CompilerParams(vmem_limit_bytes=limit),
        **more,
    )


def in_hbm(value):
    return pltpu.with_memory_space_constraint(value, pltpu.HBM)


def whole(count):
    return [pl.BlockSpec(memory_space=pltpu.VMEM)] * count


def hat(a, b):
    return jnp.maximum(TAPS - jnp.abs(a - b), 0)


def bf(value):
    return value.astype(jnp.bfloat16)


def f32(value):
    return value.astype(jnp.float32)


def parts_of(value, count):
    out = []
    for _ in range(count):
        part = bf(value)
        out.append(part)
        value = value - f32(part)
    return out


def dot(a, b, dims):
    return lax.dot_general(a, b, (dims, ((), ())), preferred_element_type=jnp.float32)


def iota(shape, dim):
    return lax.broadcasted_iota(jnp.int32, shape, dim)


def sensitivity_kernel(fwd_ref, adj_ref, weight_ref, terms_ref, fwd, adj, sems):
    copies = []
    for group in range(GROUPS):
        for which, (source, target) in enumerate(((fwd_ref, fwd), (adj_ref, adj))):
            piece = source.at[0, :, :, pl.ds(8 * group, 8)]
            copies.append(pltpu.make_async_copy(piece, target.at[group], sems.at[2 * group + which]))
            copies[-1].start()
    low = iota((8, 128), 0) < DEEP
    for pair in range(2):
        sides = []
        for group in (2 * pair, 2 * pair + 1):
            copies[2 * group].wait()
            copies[2 * group + 1].wait()
            total = None
            for component in range(3):
                real = f32(fwd[group, 0, component]) * f32(adj[group, 0, component])
                imag = f32(fwd[group, 1, component]) * f32(adj[group, 1, component])
                total = real - imag if total is None else total + (real - imag)
            sides.append((total * weight_ref[0]).reshape(128, 128))
        even, odd = (side.T.reshape(16, 8, 128) for side in sides)
        first = jnp.where(low, even, pltpu.roll(odd, DEEP, 1))
        second = jnp.where(low, pltpu.roll(even, DEEP, 1), odd)
        tiles = jnp.stack([first, second], axis=1).reshape(SLABS, 8, 128)
        terms_ref[:, 8 * pair : 8 * pair + 8, :] = tiles


def sensitivity(fwd, adj, weight):
    hbm = pl.BlockSpec(memory_space=pltpu.HBM)
    held = pltpu.VMEM((GROUPS, 2, 3, 8, 16, 128), jnp.bfloat16)
    return call(
        sensitivity_kernel,
        jax.ShapeDtypeStruct((SLABS, 16, 128), jnp.float32),
        in_specs=[hbm, hbm, pl.BlockSpec(memory_space=pltpu.SMEM)],
        out_specs=whole(1)[0],
        scratch_shapes=[held, held, pltpu.SemaphoreType.DMA((2 * GROUPS,))],
    )(in_hbm(fwd), in_hbm(adj), weight)


def middle_kernel(terms_ref, d_ref, m_ref, v_ref, out_ref, near_ref, far_ref):
    slab = SLABS - 1 - lax.axis_index("illum")
    rows, cols = iota((8, 256), 0), iota((8, 256), 1)
    near = hat(slab * DEEP + (rows & 3), cols & 127)
    band = bf(jnp.where(((rows >> 2) & 1) == (cols >> 7), near, 0).astype(jnp.float32))
    own = []
    for pair in range(2):
        dens = d_ref[16 * pair : 16 * pair + 16].reshape(256, 128)
        dens = jnp.concatenate([dens[:128], dens[128:]], axis=1)
        own.append(sum(dot(band, part, ((1,), (1,))) for part in parts_of(dens, 2)))
    both = jnp.concatenate([jnp.sum(terms_ref[...], axis=0)] + own, axis=0)
    out_ref[...] = jnp.broadcast_to(both[None], out_ref.shape)
    near_at = pl.multiple_of(24 * (1 - (lax.axis_index("gx") & 1)), 8)
    for k, ref in enumerate((d_ref, m_ref, v_ref)):
        near_ref[k] = ref[pl.ds(near_at, 8)]
        far_ref[k] = ref[pl.ds(24 - near_at, 8)]


def middle(terms, density, moment_one, moment_two):
    edge = jax.ShapeDtypeStruct((3, 8, 16, 128), jnp.float32)
    return call(
        middle_kernel,
        (jax.ShapeDtypeStruct((16, 32, 128), jnp.float32), edge, edge),
        in_specs=whole(4),
        out_specs=tuple(whole(3)),
    )(terms, density, moment_one, moment_two)


def plane_taps():
    dx, dy, x, y = np.meshgrid(np.arange(-1, 2), np.arange(-1, 2), np.arange(8), np.arange(16), indexing="ij")
    far_x = (x + 8 * dx).reshape(-1, 1) - np.repeat(np.arange(8), 16)
    far_y = (y + 16 * dy).reshape(-1, 1) - np.tile(np.arange(16), 8)
    taps = np.maximum(TAPS - np.abs(far_x), 0) * np.maximum(TAPS - np.abs(far_y), 0)
    return jnp.asarray(taps.astype(np.float32)).astype(jnp.bfloat16)


PAD_X, PAD_Y = 3, 2


def slab_kernel(all_ref, taps_ref, out_ref, sens, dens):
    gx, gy = lax.axis_index("gx"), lax.axis_index("gy")
    low = iota((8, 128), 0) < DEEP
    zero = jnp.zeros((8, 128), jnp.float32)
    for ref in (sens, dens):
        for x in range(16 + 2 * PAD_X):
            for y in range(4 + 2 * PAD_Y):
                if not (PAD_X <= x < 16 + PAD_X and PAD_Y <= y < 4 + PAD_Y):
                    ref[x, y] = zero
    for x in range(4):
        for y in range(4):
            for pair in range(2):
                at = PAD_X + 4 * x + 2 * pair
                for ref, base in ((sens, 0), (dens, 16)):
                    tile = all_ref[15 - (4 * y + x), base + 8 * pair : base + 8 * pair + 8, :]
                    turned = pltpu.roll(tile, DEEP, 0)
                    twice = (jnp.where(low, tile, turned), jnp.where(low, turned, tile))
                    for odd in range(2):
                        value = twice[odd]
                        if base:
                            top = f32(bf(value))
                            value = jnp.where(low, top, value - top)
                        ref[at + odd, PAD_Y + y] = value
    taps = taps_ref[...]
    first = GROUPS * gx
    window = dens[pl.ds(first, 10), pl.ds(gy, 5)]
    side = jnp.concatenate(
        [bf(window[dx : dx + 8, dy : dy + 3].reshape(192, 128)) for dx in range(3) for dy in range(3)], axis=1
    )
    filtered = dot(side, taps, ((1,), (0,))).reshape(24, 8, 128)
    filtered = (filtered + pltpu.roll(filtered, DEEP, 1)) * (UNIT * UNIT * UNIT)
    inner = jnp.tanh(sharpness * (filtered - threshold))
    scale = jnp.tanh(jnp.full((8, 128), sharpness * threshold, jnp.float32)) * 2.0
    slope = sharpness * (1.0 - inner * inner) / scale
    chained = slope * sens[pl.ds(first + 1, 8), pl.ds(gy + 1, 3)].reshape(24, 8, 128)
    top = f32(bf(chained))
    chained = bf(jnp.where(low, top, chained - top)).reshape(8, 3, 8, 128)
    side = jnp.concatenate([chained[dx : dx + 6, dy].reshape(48, 128) for dx in range(3) for dy in range(3)], axis=1)
    result = dot(side, taps, ((1,), (0,))).reshape(6, 8, 128)
    result = result + pltpu.roll(result, DEEP, 1)
    for pair in range(3):
        tile = jnp.where(low, result[2 * pair], result[2 * pair + 1])
        out_ref[:, 8 * pair : 8 * pair + 8, :] = jnp.broadcast_to(tile[None], (SLABS, 8, 128))


def slab_step(everything):
    return call(
        slab_kernel,
        jax.ShapeDtypeStruct((SLABS, 24, 128), jnp.float32),
        in_specs=whole(2),
        out_specs=whole(1)[0],
        scratch_shapes=[pltpu.VMEM((16 + 2 * PAD_X, 4 + 2 * PAD_Y, 8, 128), jnp.float32)] * 2,
    )(everything, plane_taps())


def adam(density, moment_one, moment_two, gradient):
    new_one = 0.9 * moment_one + 0.1 * gradient
    new_two = 0.999 * moment_two + 0.001 * gradient * gradient
    first_fix = 1.0 - 0.9**5
    second_fix = 1.0 - 0.999**5
    step = new_one / first_fix / (jnp.sqrt(new_two / second_fix) + 1e-08)
    return jnp.clip(density - 0.05 * step, 0.0, 1.0), new_one, new_two


def box(value):
    n = value.shape[0]
    two = value[: n - 1] + value[1:]
    four = two[: n - 3] + two[2:]
    eight = four[: n - 7] + four[4:]
    return eight[: n - 8] + value[8:]


def adam_kernel(slabs_ref, d_ref, m_ref, v_ref, near_ref, far_ref, nd_ref, nm_ref, nv_ref, fx_ref, ynear_ref, yfar_ref, ext):
    gx, gy = lax.axis_index("gx"), lax.axis_index("gy")
    even_x, even_y = (gx & 1) == 0, (gy & 1) == 0
    rows, cols = iota((256, 256), 0), iota((256, 256), 1)
    depth = (rows >> 3) * DEEP + (rows & 3)
    near = jnp.where(((rows >> 2) & 1) == (cols >> 7), hat(depth, cols & 127), 0)
    band = bf(near.astype(jnp.float32))
    for pair in range(3):
        side = slabs_ref[:, 8 * pair : 8 * pair + 8, :].reshape(256, 128)
        both = sum(dot(part, band, ((0,), (0,))) for part in parts_of(side, 2)) * (UNIT * UNIT * UNIT)
        for odd in range(2):
            group = 2 * pair + odd - 1
            gradient = both[:, 128 * odd : 128 * odd + 128].reshape(8, 16, 128)
            if group == -1:
                left = [jnp.where(even_x, far_ref[k], near_ref[k]) for k in range(3)]
                new, _, _ = adam(*left, gradient)
                new = jnp.where(gx > 0, new, 0.0)
            elif group == GROUPS:
                right = [jnp.where(even_x, near_ref[k], far_ref[k]) for k in range(3)]
                new, _, _ = adam(*right, gradient)
                new = jnp.where(gx < lax.axis_size("gx") - 1, new, 0.0)
            else:
                at = slice(8 * group, 8 * group + 8)
                new, one, two = adam(d_ref[at], m_ref[at], v_ref[at], gradient)
                nd_ref[at] = new
                nm_ref[at] = one
                nv_ref[at] = two
            ext[8 * (group + 1) : 8 * (group + 1) + 8] = new
    along_x = box(box(ext[...])) * UNIT
    fx_ref[...] = along_x
    low, high = along_x[:, :8], along_x[:, 8:]
    ynear_ref[...] = jnp.where(even_y, high, low)
    yfar_ref[...] = jnp.where(even_y, low, high)


def adam_step(slabs, density, moment_one, moment_two, near, far):
    tile = jax.ShapeDtypeStruct((32, 16, 128), jnp.float32)
    half = jax.ShapeDtypeStruct((32, 8, 128), jnp.float32)
    return call(
        adam_kernel,
        (tile, tile, tile, tile, half, half),
        in_specs=whole(6),
        out_specs=tuple(whole(6)),
        scratch_shapes=[pltpu.VMEM((48, 16, 128), jnp.float32)],
    )(slabs, density, moment_one, moment_two, near, far)


def yz_filter(spread, sides):
    band = bf(hat(iota((128, 128), 0), iota((128, 128), 1)).astype(jnp.float32))
    side = jnp.concatenate(sides, axis=1)
    both = sum(dot(spread, part, ((1,), (0,))) for part in parts_of(side, 2))
    for odd in range(2):
        along_y = both[:, 128 * odd : 128 * odd + 128]
        yield sum(dot(part, band, ((1,), (0,))) for part in parts_of(along_y, 2)) * (UNIT * UNIT)


def own_kernel(fx_ref, nd_ref, nm_ref, nv_ref, own_ref, nd_out, nm_out, nv_out, sems):
    copies = [
        pltpu.make_async_copy(source, target, sems.at[k])
        for k, (source, target) in enumerate(((nd_ref, nd_out), (nm_ref, nm_out), (nv_ref, nv_out)))
    ]
    for copy in copies:
        copy.start()
    rows, cols = iota((128, 128), 0), iota((128, 128), 1)
    spread = bf(jnp.where((rows >> 4) == (cols >> 4), hat(rows & 15, cols & 15), 0).astype(jnp.float32))
    for pair in range(2):
        groups = [slice(8 * g, 8 * g + 8) for g in (2 * pair, 2 * pair + 1)]
        values = yz_filter(spread, [fx_ref[at].reshape(128, 128) for at in groups])
        for at, value in zip(groups, values):
            own_ref[at] = value.reshape(8, 16, 128)
    for copy in copies:
        copy.wait()


def own_step(along_x, *results):
    tile = jax.ShapeDtypeStruct((32, 16, 128), jnp.float32)
    return call(
        own_kernel,
        (tile, tile, tile, tile),
        in_specs=whole(4),
        out_specs=tuple(whole(1) + [pl.BlockSpec(memory_space=pltpu.HBM)] * 3),
        scratch_shapes=[pltpu.SemaphoreType.DMA((3,))],
    )(along_x, *results)


def physical_kernel(far_ref, own_ref, near_ref, out_ref, held, sems):
    even = (lax.axis_index("gy") & 1) == 0
    rows, cols = iota((128, 128), 0), iota((128, 128), 1)
    later = (cols < 64) == even
    y = (cols & 7) + jnp.where(later, 16, -8)
    spread = bf(jnp.where(((cols & 63) >> 3) == (rows >> 4), hat(y, rows & 15), 0).astype(jnp.float32))
    scale = jnp.tanh(jnp.full((128, 128), sharpness * threshold, jnp.float32))
    copies = []
    for pair in range(2):
        groups = [slice(8 * g, 8 * g + 8) for g in (2 * pair, 2 * pair + 1)]
        sides = [jnp.concatenate([near_ref[at].reshape(64, 128), far_ref[at].reshape(64, 128)], axis=0) for at in groups]
        for at, value in zip(groups, yz_filter(spread, sides)):
            value = value + own_ref[at].reshape(128, 128)
            value = (scale + jnp.tanh(sharpness * (value - threshold))) / (scale + scale)
            held[at] = value.reshape(8, 16, 128)
            copies.append(pltpu.make_async_copy(held.at[at], out_ref.at[at], sems.at[len(copies)]))
            copies[-1].start()
    for copy in copies:
        copy.wait()


def physical_step(own, near, far):
    return call(
        physical_kernel,
        jax.ShapeDtypeStruct((32, 16, 128), jnp.float32),
        in_specs=whole(3),
        out_specs=pl.BlockSpec(memory_space=pltpu.HBM),
        scratch_shapes=[pltpu.VMEM((32, 16, 128), jnp.float32), pltpu.SemaphoreType.DMA((GROUPS,))],
    )(far, own, near)


def swap(near, far, axis):
    size = lax.axis_size(axis)
    pairs = [(i, i ^ 1) for i in range(size)]
    others = [(i, j) for k in range(1, size - 1, 2) for i, j in ((k, k + 1), (k + 1, k))]
    far = lax.ppermute(far, axis, others)
    return lax.ppermute(near, axis, pairs), far


def exchange(value, axes, groups=None):
    return lax.all_to_all(value, axes, 0, 0, tiled=True, axis_index_groups=groups)


def countdown(axes):
    return [list(reversed(range(lax.axis_size(axes))))]


def shards(density, moment_one, moment_two, forward_field, adjoint_field, objective_weight):
    state = (density, moment_one, moment_two)
    terms = exchange(sensitivity(forward_field, adjoint_field, objective_weight), "illum", countdown("illum"))
    both, near, far = middle(terms, *state)
    slab = slab_step(exchange(both, ("gy", "gx"), countdown(("gy", "gx"))))
    slab, near, far = lax.optimization_barrier((slab, near, far))
    slabs = exchange(slab, "illum", countdown("illum"))
    near, far = swap(near, far, "gx")
    *results, along_x, near, far = adam_step(slabs, *state, near, far)
    near, far = swap(near, far, "gy")
    own, *results = own_step(along_x, *results)
    return (*results, physical_step(own, near, far))


def solution(mesh):
    tile = P("gx", "gy", None)
    field = P("illum", None, None, "gx", "gy", None)
    return jax.shard_map(
        shards,
        mesh=mesh,
        in_specs=(tile, tile, tile, field, field, P("illum")),
        out_specs=(tile, tile, tile, tile),
        check_vma=False,
    )
```

```python
import jax
import jax.numpy as jnp
import numpy as np
from jax import lax
from jax.experimental import pallas as pl
from jax.experimental.pallas import tpu as pltpu
from jax.sharding import PartitionSpec as P

RADIUS = 8
TAPS = RADIUS + 1
UNIT = 1.0 / float(TAPS**2)
sharpness = 8.0
threshold = 0.5

GROUPS = 4
SLABS = 32
DEEP = 4


def call(kernel, out_shape, limit=48 * 1024 * 1024, **more):
    return pl.pallas_call(
        kernel,
        out_shape=out_shape,
        compiler_params=pltpu.CompilerParams(vmem_limit_bytes=limit),
        **more,
    )


def in_hbm(value):
    return pltpu.with_memory_space_constraint(value, pltpu.HBM)


def whole(count):
    return [pl.BlockSpec(memory_space=pltpu.VMEM)] * count


def hat(a, b):
    return jnp.maximum(TAPS - jnp.abs(a - b), 0)


def bf(value):
    return value.astype(jnp.bfloat16)


def f32(value):
    return value.astype(jnp.float32)


def parts_of(value, count):
    out = []
    for _ in range(count):
        part = bf(value)
        out.append(part)
        value = value - f32(part)
    return out


def dot(a, b, dims):
    return lax.dot_general(a, b, (dims, ((), ())), preferred_element_type=jnp.float32)


def iota(shape, dim):
    return lax.broadcasted_iota(jnp.int32, shape, dim)


def sensitivity_kernel(fwd_ref, adj_ref, weight_ref, terms_ref, fwd, adj, sems):
    copies = []
    for group in range(GROUPS):
        for which, (source, target) in enumerate(((fwd_ref, fwd), (adj_ref, adj))):
            piece = source.at[0, :, :, pl.ds(8 * group, 8)]
            copies.append(pltpu.make_async_copy(piece, target.at[group], sems.at[2 * group + which]))
            copies[-1].start()
    low = iota((8, 128), 0) < DEEP
    for pair in range(2):
        sides = []
        for group in (2 * pair, 2 * pair + 1):
            copies[2 * group].wait()
            copies[2 * group + 1].wait()
            total = None
            for component in range(3):
                real = f32(fwd[group, 0, component]) * f32(adj[group, 0, component])
                imag = f32(fwd[group, 1, component]) * f32(adj[group, 1, component])
                total = real - imag if total is None else total + (real - imag)
            sides.append((total * weight_ref[0]).reshape(128, 128))
        even, odd = (side.T.reshape(16, 8, 128) for side in sides)
        first = jnp.where(low, even, pltpu.roll(odd, DEEP, 1))
        second = jnp.where(low, pltpu.roll(even, DEEP, 1), odd)
        tiles = jnp.stack([first, second], axis=1).reshape(SLABS, 8, 128)
        terms_ref[:, 8 * pair : 8 * pair + 8, :] = tiles


def sensitivity(fwd, adj, weight):
    hbm = pl.BlockSpec(memory_space=pltpu.HBM)
    held = pltpu.VMEM((GROUPS, 2, 3, 8, 16, 128), jnp.bfloat16)
    return call(
        sensitivity_kernel,
        jax.ShapeDtypeStruct((SLABS, 16, 128), jnp.float32),
        in_specs=[hbm, hbm, pl.BlockSpec(memory_space=pltpu.SMEM)],
        out_specs=whole(1)[0],
        scratch_shapes=[held, held, pltpu.SemaphoreType.DMA((2 * GROUPS,))],
    )(in_hbm(fwd), in_hbm(adj), weight)


def middle_kernel(terms_ref, d_ref, m_ref, v_ref, out_ref, near_ref, far_ref):
    slab = SLABS - 1 - lax.axis_index("illum")
    rows, cols = iota((8, 256), 0), iota((8, 256), 1)
    near = hat(slab * DEEP + (rows & 3), cols & 127)
    band = bf(jnp.where(((rows >> 2) & 1) == (cols >> 7), near, 0).astype(jnp.float32))
    own = []
    for pair in range(2):
        dens = d_ref[16 * pair : 16 * pair + 16].reshape(256, 128)
        dens = jnp.concatenate([dens[:128], dens[128:]], axis=1)
        own.append(sum(dot(band, part, ((1,), (1,))) for part in parts_of(dens, 2)))
    both = jnp.concatenate([jnp.sum(terms_ref[...], axis=0)] + own, axis=0)
    out_ref[...] = jnp.broadcast_to(both[None], out_ref.shape)
    near_at = pl.multiple_of(24 * (1 - (lax.axis_index("gx") & 1)), 8)
    for k, ref in enumerate((d_ref, m_ref, v_ref)):
        near_ref[k] = ref[pl.ds(near_at, 8)]
        far_ref[k] = ref[pl.ds(24 - near_at, 8)]


def middle(terms, density, moment_one, moment_two):
    edge = jax.ShapeDtypeStruct((3, 8, 16, 128), jnp.float32)
    return call(
        middle_kernel,
        (jax.ShapeDtypeStruct((16, 32, 128), jnp.float32), edge, edge),
        in_specs=whole(4),
        out_specs=tuple(whole(3)),
    )(terms, density, moment_one, moment_two)


def plane_taps():
    dx, dy, x, y = np.meshgrid(np.arange(-1, 2), np.arange(-1, 2), np.arange(8), np.arange(16), indexing="ij")
    far_x = (x + 8 * dx).reshape(-1, 1) - np.repeat(np.arange(8), 16)
    far_y = (y + 16 * dy).reshape(-1, 1) - np.tile(np.arange(16), 8)
    taps = np.maximum(TAPS - np.abs(far_x), 0) * np.maximum(TAPS - np.abs(far_y), 0)
    return jnp.asarray(taps.astype(np.float32)).astype(jnp.bfloat16)


PAD_X, PAD_Y = 3, 2


def slab_kernel(all_ref, taps_ref, out_ref, sens, dens):
    gx, gy = lax.axis_index("gx"), lax.axis_index("gy")
    low = iota((8, 128), 0) < DEEP
    zero = jnp.zeros((8, 128), jnp.float32)
    for ref in (sens, dens):
        for x in range(16 + 2 * PAD_X):
            for y in range(4 + 2 * PAD_Y):
                if not (PAD_X <= x < 16 + PAD_X and PAD_Y <= y < 4 + PAD_Y):
                    ref[x, y] = zero
    for x in range(4):
        for y in range(4):
            for pair in range(2):
                at = PAD_X + 4 * x + 2 * pair
                for ref, base in ((sens, 0), (dens, 16)):
                    tile = all_ref[15 - (4 * y + x), base + 8 * pair : base + 8 * pair + 8, :]
                    turned = pltpu.roll(tile, DEEP, 0)
                    twice = (jnp.where(low, tile, turned), jnp.where(low, turned, tile))
                    for odd in range(2):
                        value = twice[odd]
                        if base:
                            top = f32(bf(value))
                            value = jnp.where(low, top, value - top)
                        ref[at + odd, PAD_Y + y] = value
    taps = taps_ref[...]
    first = GROUPS * gx
    window = dens[pl.ds(first, 10), pl.ds(gy, 5)]
    side = jnp.concatenate(
        [bf(window[dx : dx + 8, dy : dy + 3].reshape(192, 128)) for dx in range(3) for dy in range(3)], axis=1
    )
    filtered = dot(side, taps, ((1,), (0,))).reshape(24, 8, 128)
    filtered = (filtered + pltpu.roll(filtered, DEEP, 1)) * (UNIT * UNIT * UNIT)
    inner = jnp.tanh(sharpness * (filtered - threshold))
    scale = jnp.tanh(jnp.full((8, 128), sharpness * threshold, jnp.float32)) * 2.0
    slope = sharpness * (1.0 - inner * inner) / scale
    chained = slope * sens[pl.ds(first + 1, 8), pl.ds(gy + 1, 3)].reshape(24, 8, 128)
    top = f32(bf(chained))
    chained = bf(jnp.where(low, top, chained - top)).reshape(8, 3, 8, 128)
    side = jnp.concatenate([chained[dx : dx + 6, dy].reshape(48, 128) for dx in range(3) for dy in range(3)], axis=1)
    result = dot(side, taps, ((1,), (0,))).reshape(6, 8, 128)
    result = result + pltpu.roll(result, DEEP, 1)
    for pair in range(3):
        tile = jnp.where(low, result[2 * pair], result[2 * pair + 1])
        out_ref[:, 8 * pair : 8 * pair + 8, :] = jnp.broadcast_to(tile[None], (SLABS, 8, 128))


def slab_step(everything):
    return call(
        slab_kernel,
        jax.ShapeDtypeStruct((SLABS, 24, 128), jnp.float32),
        in_specs=whole(2),
        out_specs=whole(1)[0],
        scratch_shapes=[pltpu.VMEM((16 + 2 * PAD_X, 4 + 2 * PAD_Y, 8, 128), jnp.float32)] * 2,
    )(everything, plane_taps())


def adam(density, moment_one, moment_two, gradient):
    new_one = 0.9 * moment_one + 0.1 * gradient
    new_two = 0.999 * moment_two + 0.001 * gradient * gradient
    first_fix = 1.0 - 0.9**5
    second_fix = 1.0 - 0.999**5
    step = new_one / first_fix / (jnp.sqrt(new_two / second_fix) + 1e-08)
    return jnp.clip(density - 0.05 * step, 0.0, 1.0), new_one, new_two


def box(value):
    n = value.shape[0]
    two = value[: n - 1] + value[1:]
    four = two[: n - 3] + two[2:]
    eight = four[: n - 7] + four[4:]
    return eight[: n - 8] + value[8:]


def adam_kernel(slabs_ref, d_ref, m_ref, v_ref, near_ref, far_ref, nd_ref, nm_ref, nv_ref, fx_ref, ynear_ref, yfar_ref, ext):
    gx, gy = lax.axis_index("gx"), lax.axis_index("gy")
    even_x, even_y = (gx & 1) == 0, (gy & 1) == 0
    rows, cols = iota((256, 256), 0), iota((256, 256), 1)
    depth = (SLABS - 1 - (rows >> 3)) * DEEP + (rows & 3)
    near = jnp.where(((rows >> 2) & 1) == (cols >> 7), hat(depth, cols & 127), 0)
    band = bf(near.astype(jnp.float32))
    for pair in range(3):
        side = slabs_ref[:, 8 * pair : 8 * pair + 8, :].reshape(256, 128)
        both = sum(dot(part, band, ((0,), (0,))) for part in parts_of(side, 2)) * (UNIT * UNIT * UNIT)
        for odd in range(2):
            group = 2 * pair + odd - 1
            gradient = both[:, 128 * odd : 128 * odd + 128].reshape(8, 16, 128)
            if group == -1:
                left = [jnp.where(even_x, far_ref[k], near_ref[k]) for k in range(3)]
                new, _, _ = adam(*left, gradient)
                new = jnp.where(gx > 0, new, 0.0)
            elif group == GROUPS:
                right = [jnp.where(even_x, near_ref[k], far_ref[k]) for k in range(3)]
                new, _, _ = adam(*right, gradient)
                new = jnp.where(gx < lax.axis_size("gx") - 1, new, 0.0)
            else:
                at = slice(8 * group, 8 * group + 8)
                new, one, two = adam(d_ref[at], m_ref[at], v_ref[at], gradient)
                nd_ref[at] = new
                nm_ref[at] = one
                nv_ref[at] = two
            ext[8 * (group + 1) : 8 * (group + 1) + 8] = new
    along_x = box(box(ext[...])) * UNIT
    fx_ref[...] = along_x
    low, high = along_x[:, :8], along_x[:, 8:]
    ynear_ref[...] = jnp.where(even_y, high, low)
    yfar_ref[...] = jnp.where(even_y, low, high)


def adam_step(slabs, density, moment_one, moment_two, near, far):
    tile = jax.ShapeDtypeStruct((32, 16, 128), jnp.float32)
    half = jax.ShapeDtypeStruct((32, 8, 128), jnp.float32)
    return call(
        adam_kernel,
        (tile, tile, tile, tile, half, half),
        in_specs=whole(6),
        out_specs=tuple(whole(6)),
        scratch_shapes=[pltpu.VMEM((48, 16, 128), jnp.float32)],
    )(slabs, density, moment_one, moment_two, near, far)


def yz_filter(spread, sides):
    band = bf(hat(iota((128, 128), 0), iota((128, 128), 1)).astype(jnp.float32))
    side = jnp.concatenate(sides, axis=1)
    both = sum(dot(spread, part, ((1,), (0,))) for part in parts_of(side, 2))
    for odd in range(2):
        along_y = both[:, 128 * odd : 128 * odd + 128]
        yield sum(dot(part, band, ((1,), (0,))) for part in parts_of(along_y, 2)) * (UNIT * UNIT)


def own_kernel(fx_ref, nd_ref, nm_ref, nv_ref, own_ref, nd_out, nm_out, nv_out, sems):
    copies = [
        pltpu.make_async_copy(source, target, sems.at[k])
        for k, (source, target) in enumerate(((nd_ref, nd_out), (nm_ref, nm_out), (nv_ref, nv_out)))
    ]
    for copy in copies:
        copy.start()
    rows, cols = iota((128, 128), 0), iota((128, 128), 1)
    spread = bf(jnp.where((rows >> 4) == (cols >> 4), hat(rows & 15, cols & 15), 0).astype(jnp.float32))
    for pair in range(2):
        groups = [slice(8 * g, 8 * g + 8) for g in (2 * pair, 2 * pair + 1)]
        values = yz_filter(spread, [fx_ref[at].reshape(128, 128) for at in groups])
        for at, value in zip(groups, values):
            own_ref[at] = value.reshape(8, 16, 128)
    for copy in copies:
        copy.wait()


def own_step(along_x, *results):
    tile = jax.ShapeDtypeStruct((32, 16, 128), jnp.float32)
    return call(
        own_kernel,
        (tile, tile, tile, tile),
        in_specs=whole(4),
        out_specs=tuple(whole(1) + [pl.BlockSpec(memory_space=pltpu.HBM)] * 3),
        scratch_shapes=[pltpu.SemaphoreType.DMA((3,))],
    )(along_x, *results)


def physical_kernel(far_ref, own_ref, near_ref, out_ref, held, sems):
    even = (lax.axis_index("gy") & 1) == 0
    rows, cols = iota((128, 128), 0), iota((128, 128), 1)
    later = (cols < 64) == even
    y = (cols & 7) + jnp.where(later, 16, -8)
    spread = bf(jnp.where(((cols & 63) >> 3) == (rows >> 4), hat(y, rows & 15), 0).astype(jnp.float32))
    scale = jnp.tanh(jnp.full((128, 128), sharpness * threshold, jnp.float32))
    copies = []
    for pair in range(2):
        groups = [slice(8 * g, 8 * g + 8) for g in (2 * pair, 2 * pair + 1)]
        sides = [jnp.concatenate([near_ref[at].reshape(64, 128), far_ref[at].reshape(64, 128)], axis=0) for at in groups]
        for at, value in zip(groups, yz_filter(spread, sides)):
            value = value + own_ref[at].reshape(128, 128)
            value = (scale + jnp.tanh(sharpness * (value - threshold))) / (scale + scale)
            held[at] = value.reshape(8, 16, 128)
            copies.append(pltpu.make_async_copy(held.at[at], out_ref.at[at], sems.at[len(copies)]))
            copies[-1].start()
    for copy in copies:
        copy.wait()


def physical_step(own, near, far):
    return call(
        physical_kernel,
        jax.ShapeDtypeStruct((32, 16, 128), jnp.float32),
        in_specs=whole(3),
        out_specs=pl.BlockSpec(memory_space=pltpu.HBM),
        scratch_shapes=[pltpu.VMEM((32, 16, 128), jnp.float32), pltpu.SemaphoreType.DMA((GROUPS,))],
    )(far, own, near)


def swap(near, far, axis):
    size = lax.axis_size(axis)
    pairs = [(i, i ^ 1) for i in range(size)]
    others = [(i, j) for k in range(1, size - 1, 2) for i, j in ((k, k + 1), (k + 1, k))]
    far = lax.ppermute(far, axis, others)
    return lax.ppermute(near, axis, pairs), far


def exchange(value, axes, groups=None):
    return lax.all_to_all(value, axes, 0, 0, tiled=True, axis_index_groups=groups)


def countdown(axes):
    return [list(reversed(range(lax.axis_size(axes))))]


def shards(density, moment_one, moment_two, forward_field, adjoint_field, objective_weight):
    state = (density, moment_one, moment_two)
    terms = exchange(sensitivity(forward_field, adjoint_field, objective_weight), "illum", countdown("illum"))
    both, near, far = middle(terms, *state)
    slab = slab_step(exchange(both, ("gy", "gx"), countdown(("gy", "gx"))))
    slab, near, far = lax.optimization_barrier((slab, near, far))
    slabs = exchange(slab, "illum")
    near, far = swap(near, far, "gx")
    *results, along_x, near, far = adam_step(slabs, *state, near, far)
    near, far = swap(near, far, "gy")
    own, *results = own_step(along_x, *results)
    return (*results, physical_step(own, near, far))


def solution(mesh):
    tile = P("gx", "gy", None)
    field = P("illum", None, None, "gx", "gy", None)
    return jax.shard_map(
        shards,
        mesh=mesh,
        in_specs=(tile, tile, tile, field, field, P("illum")),
        out_specs=(tile, tile, tile, tile),
        check_vma=False,
    )
```
